256 devices in a mesh: scen: 16 (over z_hi, y, core), grp: 16 (over x, z_lo).
Axes of the slice: x: 4, y: 4, z: 8 (z_hi: 2, z_lo: 4; z = z_hi * 4 + z_lo), core: 2. Of those that a mesh axis runs over, the one named last changes fastest.
Arguments:
- linking: bfloat16 [32, 1024, 4096], P('scen', None, 'grp'), may hold values from -6 to 6
- reach_count: int32 [32], P('scen'), may hold values from 1 to 4, as said below
- diag_inverse: bfloat16 [32, 4, 256, 256], P('scen', None, 'grp'), as said below
- off_blocks: bfloat16 [32, 4, 2, 256, 256], P('scen', None, None, 'grp'), may hold values from -0.1875 to 0.1875
- targets: int32 [32, 4, 2], P('scen'), may hold values from 1 to 4, as said below
Outputs:
- schur: float32 [4096, 4096], P('grp', 'scen')
The draws below stay inside these ranges and needn't reach their ends.
Inputs may be any that keep to these rules, and one draw needn't show every extreme that they name: Only the last reach_count[s] supernodes of scenario s take part; some scenario has all 4. `targets`: the 2 entries of row [s, j] are distinct supernodes above j, or 4 for an unused slot. `diag_inverse`: each block is lower triangular with a positive diagonal.
All inputs are finite; a program needn't handle non-finite values.
Results may differ from the reference program's by a relative error of at most 0.003.
Values may be sent and summed in bfloat16 or wider, within the bound.
A program may use at most 192 MiB of HBM per device.

```python
import math
import jax
import jax.numpy as jnp
from jax import lax

SB = 256
NS = 4
P_SIZE = 2
LINK = 4096
SCEN = 32
NROWS = 1024


def draw_reach_count(key, part):
    key = jax.random.fold_in(key, 11)
    first_key, second_key = jax.random.split(key)
    counts = jax.random.randint(first_key, (SCEN,), 1, NS + 1)
    chosen = jax.random.randint(second_key, (), 0, SCEN)
    return jnp.where(jnp.arange(SCEN) == chosen, NS, counts).astype(jnp.int32)


def draw_targets(key, part):
    key = jax.random.fold_in(key, 12)
    scores = jax.random.randint(key, (SCEN, NS, NS), 0, 2 ** 20) * NS + jnp.arange(NS)[None, None, :]
    invalid = jnp.arange(NS)[None, None, :] <= jnp.arange(NS)[None, :, None]
    scores = jnp.where(invalid, scores + 2 ** 26, scores)
    order = jnp.argsort(scores, axis=-1)[:, :, :P_SIZE]
    valid = order > jnp.arange(NS)[None, :, None]
    return jnp.where(valid, order, NS).astype(jnp.int32)


def draw_diag_inverse(key, part):
    key = jax.random.fold_in(key, 13)
    first_key, second_key = jax.random.split(key)
    shape = (SCEN, NS, SB, SB)
    diagonal = jax.random.uniform(first_key, shape, jnp.float32, 0.7, 1.4)
    lower = jax.random.normal(second_key, shape, jnp.float32) * (0.5 / SB ** 0.5)
    rows = jnp.arange(SB)[:, None]
    cols = jnp.arange(SB)[None, :]
    value = jnp.where(rows == cols, diagonal, jnp.where(rows > cols, lower, 0.0))
    return value.astype(jnp.bfloat16)


def strengthened(array, stream_key, source, target, shards_of, factor):
    def block_of(position):
        return (jnp.arange(array.shape[position]) // (array.shape[position] // shards_of)).reshape((-1,) + (1,) * (array.ndim - 1 - position))

    one_side = jax.random.permutation(stream_key, shards_of)[block_of(target)]
    second = (block_of(target) + shards_of // 2) % shards_of
    return jnp.where((block_of(source) == one_side) | (block_of(source) == second), factor * array, array)


def block_scale(key, dims, cuts, low, high):
    factor_of, own = 1.0, jax.random.fold_in(key, 6)
    for position, shards_of in cuts:
        draws = jnp.exp(jax.random.uniform(jax.random.fold_in(own, position), (shards_of,), jnp.float32, low / len(cuts), high / len(cuts)))
        factor_of = factor_of * jnp.repeat(draws, dims[position] // shards_of).reshape([-1 if axis == position else 1 for axis in range(len(dims))])
    return factor_of


def noise(key, dims, spread, most, cuts=(), kind=jnp.bfloat16):
    level = block_scale(key, dims, cuts, -0.22, 0.18) if cuts else 1.0
    values = jax.random.normal(key, dims, jnp.float32) * spread * level
    return jnp.minimum(jnp.maximum(values, -most), most).astype(kind)


def heavy_noise(own_key, shape, width, reach, shards, heavy, kind=jnp.bfloat16):
    result = width * jax.random.normal(own_key, shape, jnp.float32)
    if shards:
        result = result * block_scale(own_key, shape, shards, -0.22, 0.18)
    return jnp.clip(strengthened(result, jax.random.fold_in(own_key, 3), *heavy), -reach, reach).astype(kind)


def setup_inputs(seed: int = 0) -> dict:
    streams_of = jax.random.split(jax.random.key(seed), 6)
    linking = heavy_noise(streams_of[0], (SCEN, NROWS, LINK), 1.0, 6.0, ((0, 16), (2, 16)), (0, 2, 16, 2.0))
    reach_count = draw_reach_count(jax.random.fold_in(streams_of[5], 71), 0)
    diag_inverse = draw_diag_inverse(jax.random.fold_in(streams_of[5], 71), 0)
    off_blocks = noise(streams_of[3], (SCEN, NS, P_SIZE, SB, SB), (4 * SB) ** -0.5, 0.1875, ((0, 16), (3, 16)))
    targets = draw_targets(jax.random.fold_in(streams_of[5], 71), 0)
    return {"linking": linking, "reach_count": reach_count, "diag_inverse": diag_inverse, "off_blocks": off_blocks, "targets": targets}


def reference(linking, reach_count, diag_inverse, off_blocks, targets):
    node_ids = jnp.arange(NS, dtype=jnp.int32)

    def one_scenario(total, items):
        columns, count, inverses, lower_blocks, target_rows = items
        columns = columns.reshape(NS, SB, LINK)
        first = NS - count
        keep = node_ids >= first
        active = jnp.where(keep[:, None, None], columns, jnp.zeros_like(columns))
        pending = jnp.zeros((NS, SB, LINK), jnp.float32)
        solved_list = []
        for node in range(NS):
            residual = (active[node].astype(jnp.float32) - pending[node]).astype(jnp.bfloat16)
            solved_block = jnp.dot(inverses[node], residual, preferred_element_type=jnp.float32).astype(jnp.bfloat16)
            for slot in range(P_SIZE):
                update = jnp.dot(lower_blocks[node, slot], solved_block, preferred_element_type=jnp.float32)
                match = node_ids == target_rows[node, slot]
                pending = pending + jnp.where(match[:, None, None], update[None], jnp.zeros_like(update)[None])
            solved_list.append(solved_block)
        solved = jnp.concatenate(solved_list, axis=0)
        total = total + lax.dot_general(solved, solved, (((0,), (0,)), ((), ())), preferred_element_type=jnp.float32)
        return (total, None)
    total, unused = lax.scan(one_scenario, jnp.zeros((LINK, LINK), jnp.float32), (linking, reach_count, diag_inverse, off_blocks, targets))
    return total * (1.0 / math.sqrt(SCEN * NROWS))
```

```python
import math

import jax
import jax.numpy as jnp
from jax import lax
from jax.experimental import pallas as pl
from jax.experimental.pallas import tpu as pltpu
from jax.sharding import PartitionSpec as P

F32 = jnp.float32
BF16 = jnp.bfloat16
MESH = pl.DeviceIdType.MESH

NX = 4
NZ = 4
NY = 4
SB = 256
NS = 4
ROWS = NS * SB
HALF = ROWS // 2
PACK = 9
REL = (0, 1, 3, 2)

BATCHES = (
    ((3, 0), (3, 1), (3, 2), (0, 0), (0, 1), (0, 2)),
    ((1, 0), (1, 1), (1, 2), (2, 0), (2, 1), (2, 2)),
    ((3, 3), (0, 3), (1, 3), (2, 3)),
)
STARTS = (0, 6, 12)
OTHERS = ((0,), (1, 2), (0, 1, 2))
WIDTH = ((0, 1, 2), (0, 1, 2), (3,))
TILES = 16


def send(src, dst, send_sem, recv_sem, device):
    pltpu.make_async_remote_copy(
        src_ref=src,
        dst_ref=dst,
        send_sem=send_sem,
        recv_sem=recv_sem,
        device_id=device,
        device_id_type=MESH,
    ).start()


def await_bytes(ref, sem):
    pltpu.make_async_copy(ref, ref, sem).wait()


def flag(condition):
    return jnp.where(condition, 1.0, 0.0).astype(F32)


def mm(a, b):
    return lax.dot_general(a, b, (((1,), (1,)), ((), ())), preferred_element_type=F32)


def kernel(
    scaling,
    targets_hbm,
    reach_hbm,
    linking_hbm,
    diag,
    off,
    out,
    targets,
    reach,
    linking,
    choice,
    factors,
    lower,
    columns,
    solved,
    raw_z,
    solved_z,
    partial,
    from_core,
    to_y,
    from_y,
    reduced,
    near_z,
    near_x,
    slices,
    final,
    in_s,
    fz_s,
    fz_r,
    fx_s,
    fx_r,
    ff_s,
    ff_r,
    sx_s,
    sx_r,
    zl_s,
    zl_r,
    c_s,
    c_r,
    y_s,
    y_r,
    nz_s,
    nz_r,
    nx_s,
    nx_r,
    fn_s,
    fn_r,
):
    s = lax.axis_index("scen")
    g = lax.axis_index("grp")
    x, z = g // NZ, g % NZ
    core, y, z_hi = s % 2, (s // 2) % NY, s // (2 * NY)
    right_x, left_x, far_x = (x + 1) % NX, (x + 3) % NX, (x + 2) % NX
    right = (s, right_x * NZ + z)
    left = (s, left_x * NZ + z)
    upper = z // 2
    places = (z + 1 - 2 * (z % 2), 2 - upper, 3 - 3 * upper, z)

    def at_x(i):
        return (x + REL[i]) % NX

    barrier = pltpu.get_barrier_semaphore()

    def greet(k, carry):
        pl.semaphore_signal(barrier, inc=1, device_id=((s + k) % 16, g), device_id_type=MESH)
        return carry

    lax.fori_loop(1, 16, greet, 0)
    for k in range(1, NZ):
        pl.semaphore_signal(barrier, inc=1, device_id=(s, x * NZ + (z + k) % NZ), device_id_type=MESH)
    for k in range(1, NX):
        pl.semaphore_signal(barrier, inc=1, device_id=(s, ((x + k) % NX) * NZ + z), device_id_type=MESH)

    fetches = [(targets_hbm, targets), (reach_hbm, reach)]
    for sc in range(2):
        fetches.append((off.at[sc, 2], choice.at[sc]))
        fetches.append((diag.at[sc], factors.at[sc, g, pl.ds(0, NS)]))
        for i in range(2):
            fetches.append((off.at[sc, i], factors.at[sc, g, pl.ds(NS + 2 * i, 2)]))
    fetches.append((linking_hbm, linking))
    copies = [pltpu.make_async_copy(a, b, in_s.at[n]) for n, (a, b) in enumerate(fetches)]
    for copy in copies:
        copy.start()
    for copy in copies[:-1]:
        copy.wait()
    for sc in range(2):
        first = choice[sc, 0].astype(F32) * flag(targets[sc, 0, 2] == 3)
        second = choice[sc, 1].astype(F32) * flag(targets[sc, 1, 2] == 3)
        factors[sc, g, 8] = (first + second).astype(BF16)

    pl.semaphore_wait(barrier, 21)

    def shard(sc, xx, k):
        return factors.at[sc, xx * NZ + (z + k) % NZ]

    def x_send(sc, k):
        piece = shard(sc, x, k)
        send(piece, piece, fx_s.at[sc, 0, k], fx_r.at[sc, 0, k], right)
        send(piece, piece, fx_s.at[sc, 1, k], fx_r.at[sc, 1, k], left)

    def goes_on(q):
        return ((q < z) & (z < NZ - 1), (q > z) & (z > 0))

    def z_take(sc, o):
        q = places[o]
        piece = factors.at[sc, x * NZ + q]
        await_bytes(piece, fz_r.at[sc, q])
        for onward, device in zip(goes_on(q), ((s, g + 1), (s, g - 1))):

            @pl.when(onward)
            def _(device=device):
                send(piece, piece, fz_s.at[sc, 2 + o], fz_r.at[sc, q], device)

        x_send(sc, (q + NZ - z) % NZ)

    def pass_right(sc, k):
        piece = shard(sc, left_x, k)
        await_bytes(piece, fx_r.at[sc, 0, k])
        send(piece, piece, ff_s.at[sc, 0, k], ff_r.at[sc, 0, k], right)

    def pass_left(sc, k):
        piece = shard(sc, right_x, k)
        await_bytes(piece, fx_r.at[sc, 1, k])
        send(piece, piece, ff_s.at[sc, 1, k], ff_r.at[sc, 1, k], left)

    def rest(sc):
        for k in (1, 2):
            await_bytes(shard(sc, left_x, k), fx_r.at[sc, 0, k])
            await_bytes(shard(sc, far_x, k), ff_r.at[sc, 1, k])
        for k in (0, 3):
            await_bytes(shard(sc, right_x, k), fx_r.at[sc, 1, k])
            await_bytes(shard(sc, far_x, k), ff_r.at[sc, 0, k])

    def z_send(sc):
        own = factors.at[sc, g]

        @pl.when(z < NZ - 1)
        def _():
            send(own, own, fz_s.at[sc, 0], fz_r.at[sc, z], (s, g + 1))

        @pl.when(z > 0)
        def _():
            send(own, own, fz_s.at[sc, 1], fz_r.at[sc, z], (s, g - 1))

        x_send(sc, 0)

    def prepare(sc):
        for i in range(3):
            for j in range(i + 1, NS):
                if i == 2:
                    block = factors[sc, :, 8].reshape(SB, SB)
                else:
                    block = jnp.zeros((SB, SB), BF16)
                    for p in range(2):
                        chosen = flag(targets[sc, p, i] == j).astype(BF16)
                        block = block + factors[sc, :, 4 + 2 * i + p].reshape(SB, SB) * chosen
                lower[sc, j - 1, :, i * SB : (i + 1) * SB] = block

    def solve(sc, source, target, own=False, after=None):
        for j in range(NS):
            if own and j == 1:
                prepare(sc)
            here = slice(j * SB, (j + 1) * SB)
            residual = source[:, here].astype(F32) * flag(j >= NS - reach[sc])
            if j:
                residual = residual - mm(target[:, : j * SB], lower[sc, j - 1, :, : j * SB])
            inverse = factors[sc, :, j].reshape(SB, SB)
            target[:, here] = mm(residual.astype(BF16), inverse).astype(BF16)
            if after is not None:
                after(j)

    def x_part(sc, i, form, first=0, count=SB):
        return solved.at[sc, i, pl.ds(first, count), pl.ds(form * HALF, HALF)]

    def solve_own(sc):
        def after(j):
            if j % 2:
                form = j // 2
                own = x_part(sc, 0, form)
                send(own, x_part(sc, 2, form), sx_s.at[sc, form, 0], sx_r.at[sc, form, 0], right)
                send(own, x_part(sc, 1, form), sx_s.at[sc, form, 1], sx_r.at[sc, form, 1], left)

        solve(sc, columns.at[sc], solved.at[sc, 0], True, after)

    def pass_x(sc, form):
        await_bytes(x_part(sc, 2, form), sx_r.at[sc, form, 0])
        send(
            x_part(sc, 2, form, 0, SB // 2),
            x_part(sc, 3, form, 0, SB // 2),
            sx_s.at[sc, form, 2],
            sx_r.at[sc, form, 2],
            right,
        )
        await_bytes(x_part(sc, 1, form), sx_r.at[sc, form, 1])
        send(
            x_part(sc, 1, form, SB // 2, SB // 2),
            x_part(sc, 3, form, SB // 2, SB // 2),
            sx_s.at[sc, form, 3],
            sx_r.at[sc, form, 3],
            left,
        )

    def far(sc, form):
        for n in range(2):
            await_bytes(x_part(sc, 3, form, n * (SB // 2), SB // 2), sx_r.at[sc, form, 2 + n])

    def z_half(ref, h):
        return ref.at[pl.ds(h * (SB // 2), SB // 2)]

    def start_z():
        for h in range(2):

            @pl.when(z < NZ - 1)
            def _(h=h):
                send(z_half(columns.at[0], h), z_half(raw_z.at[z], h), zl_s.at[0, 0, h], zl_r.at[0, 0, h], (s, g + 1))

            @pl.when(z > 0)
            def _(h=h):
                send(z_half(columns.at[1], h), z_half(raw_z.at[z], h), zl_s.at[1, 0, h], zl_r.at[1, 0, h], (s, g - 1))

    def pass_z(k):
        for h in range(2):

            @pl.when(z - k >= 0)
            def _(h=h):
                block = z_half(raw_z.at[z - k], h)
                await_bytes(block, zl_r.at[0, k - 1, h])
                if k < NZ - 1:

                    @pl.when(z < NZ - 1)
                    def _():
                        send(block, block, zl_s.at[0, k, h], zl_r.at[0, k, h], (s, g + 1))

            @pl.when(z + k <= NZ - 1)
            def _(h=h):
                block = z_half(raw_z.at[z + k], h)
                await_bytes(block, zl_r.at[1, k - 1, h])
                if k < NZ - 1:

                    @pl.when(z > 0)
                    def _():
                        send(block, block, zl_s.at[1, k, h], zl_r.at[1, k, h], (s, g - 1))

    def solve_z(o):
        sc = (1 - z % 2) if o == 0 else (1 - upper)
        solve(sc, raw_z.at[places[o]], solved_z.at[places[o]])

    z_send(0)
    z_send(1)
    copies[-1].wait()
    for sc in range(2):
        for j in range(NS):
            block = linking[sc, j * SB : (j + 1) * SB, :].astype(F32)
            columns[sc, :, j * SB : (j + 1) * SB] = block.T.astype(BF16)
    z_take(0, 0)
    pass_right(0, 0)
    pass_right(1, 0)
    z_take(1, 0)
    z_take(0, 1)
    z_take(1, 1)
    z_take(0, 2)
    z_take(1, 2)
    start_z()
    pass_left(0, 1)
    pass_left(0, 2)
    pass_right(0, 3)
    pass_left(1, 1)
    pass_right(1, 3)
    pass_left(1, 2)
    rest(0)
    solve_own(0)
    pass_z(1)
    rest(1)
    solve_own(1)

    def store(n, tile):
        partial[0, n] = tile[: SB // 2]
        partial[1, n] = tile[SB // 2 :]

    def wide(sc):
        return solved[sc, 0:3].reshape(3 * SB, ROWS)

    def store_wide(n, product, axis):
        for i in range(3):
            store(n + i, lax.slice_in_dim(product, i * SB, (i + 1) * SB, axis=axis))

    def pair(first):
        return solved_z[first : first + 2].reshape(2 * SB, ROWS)

    def gram(batch):
        near_below = z % 2 == 1
        below = upper == 1
        if batch == 0:
            store_wide(0, mm(solved[0, 0], wide(0)) + mm(solved[1, 0], wide(1)), 1)

            @pl.when(near_below)
            def _():
                store_wide(3, mm(solved_z[places[0]], wide(0)), 1)

            @pl.when(jnp.logical_not(near_below))
            def _():
                store_wide(3, mm(wide(1), solved_z[places[0]]), 0)
        elif batch == 1:
            @pl.when(below)
            def _():
                product = mm(pair(0), wide(0))
                store_wide(6, product[SB:], 1)
                store_wide(9, product[:SB], 1)

            @pl.when(jnp.logical_not(below))
            def _():
                product = mm(wide(1), pair(2))
                store_wide(6, product[:, :SB], 0)
                store_wide(9, product[:, SB:], 0)
        else:
            store(12, mm(solved[0, 0], solved[0, 3]) + mm(solved[1, 0], solved[1, 3]))

            @pl.when(near_below)
            def _():
                store(13, mm(solved_z[places[0]], solved[0, 3]))

            @pl.when(jnp.logical_not(near_below))
            def _():
                store(13, mm(solved[1, 3], solved_z[places[0]]))

            @pl.when(below)
            def _():
                product = mm(pair(0), solved[0, 3])
                store(14, product[SB:])
                store(15, product[:SB])

            @pl.when(jnp.logical_not(below))
            def _():
                product = mm(solved[1, 3], pair(2))
                store(14, product[:, :SB])
                store(15, product[:, SB:])

    def span(batch):
        return pl.ds(STARTS[batch], len(BATCHES[batch]))

    def to_core(batch):
        send(
            partial.at[1 - core, span(batch)],
            from_core.at[span(batch)],
            c_s.at[batch],
            c_r.at[batch],
            (s + 1 - 2 * core, g),
        )

    def of_y(yy, first=0, count=32):
        return pl.ds(pl.multiple_of((yy % NY) * 32 + first, 16), count)

    def both_cores(n, rows):
        return partial[core, n, rows, :] + from_core[n, rows, :]

    def over_tiles(batch, body):
        def step(n, carry):
            body(n)
            return carry

        lax.fori_loop(STARTS[batch], STARTS[batch] + len(BATCHES[batch]), step, 0)

    def along_y(batch):
        tiles = span(batch)
        await_bytes(from_core.at[tiles], c_r.at[batch])
        for k in (2, 1, 3):

            def body(n, k=k):
                to_y[k - 1, n] = both_cores(n, of_y(y + k)).astype(BF16)

            over_tiles(batch, body)
            send(
                to_y.at[k - 1, tiles],
                from_y.at[k - 1, tiles],
                y_s.at[batch, k - 1],
                y_r.at[batch, k - 1],
                (z_hi * 8 + ((y + k) % NY) * 2 + core, g),
            )

    def finish_y(batch):
        tiles = span(batch)
        for k in range(1, NY):
            await_bytes(from_y.at[k - 1, tiles], y_r.at[batch, k - 1])
        for n, (o, i) in enumerate(BATCHES[batch], STARTS[batch]):
            value = both_cores(n, of_y(y))
            for k in range(1, NY):
                value += from_y[k - 1, n].astype(F32)
            value = value.astype(BF16)
            if o == 3:
                slices[3, i] = value
            else:
                reduced[o, i] = value
                if i == 0:
                    near_x[0, o] = value

    def batch_z(ref, place, batch):
        return ref.at[place, pl.ds(WIDTH[batch][0], len(WIDTH[batch]))]

    def batch_x(ref, place, batch):
        return ref.at[place, pl.ds(OTHERS[batch][0], len(OTHERS[batch]))]

    def to_groups(batch):
        for o in OTHERS[batch]:
            send(
                batch_z(reduced, o, batch),
                batch_z(near_z, z, batch),
                nz_s.at[batch, o],
                nz_r.at[batch, z],
                (s, x * NZ + places[o]),
            )
        for i in WIDTH[batch]:
            if i:
                back = (0, 2, 1, 3)[i]
                send(
                    reduced.at[pl.ds(OTHERS[batch][0], len(OTHERS[batch])), i],
                    batch_x(near_x, back, batch),
                    nx_s.at[batch, i - 1],
                    nx_r.at[batch, back - 1],
                    (s, at_x(i) * NZ + z),
                )

    def from_groups(batch):
        for o in OTHERS[batch]:
            await_bytes(batch_z(near_z, places[o], batch), nz_r.at[batch, places[o]])
        for i in WIDTH[batch]:
            if i:
                await_bytes(batch_x(near_x, i, batch), nx_r.at[batch, i - 1])
        for o in OTHERS[batch]:
            for i in WIDTH[batch]:
                deliver(o, i)

    out_rows = pl.ds(pl.multiple_of(core * 128 + y * 32, 32), 32)

    def deliver(o, i):
        if o < 3:
            both = near_z[places[o], i].astype(F32) + near_x[i, o].astype(F32)
            slices[o, i] = both.astype(BF16)
        b = at_x(i) * NZ + places[o]
        piece = slices.at[o, i]
        target = final.at[z_hi, out_rows]

        @pl.when(b == s)
        def _():
            pltpu.make_async_copy(piece, target, fn_r.at[0]).start()

        @pl.when(b != s)
        def _():
            send(piece, target, fn_s.at[o * 4 + i], fn_r.at[0], (b, g))

    solve_z(0)
    pass_z(2)
    pass_x(0, 0)
    pass_x(0, 1)
    pass_x(1, 0)
    pass_x(1, 1)
    gram(0)
    to_core(0)
    solve_z(1)
    pass_z(3)
    along_y(0)
    solve_z(2)
    gram(1)
    to_core(1)
    far(0, 0)
    far(0, 1)
    along_y(1)
    far(1, 0)
    far(1, 1)
    gram(2)
    to_core(2)
    finish_y(0)
    to_groups(0)
    along_y(2)
    from_groups(0)
    finish_y(1)
    to_groups(1)
    finish_y(2)
    to_groups(2)
    for i in range(3):
        deliver(3, i)
    from_groups(1)
    deliver(3, 3)
    from_groups(2)

    for sc in range(2):

        @pl.when(z < NZ - 1)
        def _(sc=sc):
            await_bytes(factors.at[sc, g], fz_s.at[sc, 0])

        @pl.when(z > 0)
        def _(sc=sc):
            await_bytes(factors.at[sc, g], fz_s.at[sc, 1])

        for o in range(3):
            for onward in goes_on(places[o]):

                @pl.when(onward)
                def _(sc=sc, o=o):
                    await_bytes(factors.at[sc, g], fz_s.at[sc, 2 + o])

        for d in range(2):
            for k in range(4):
                await_bytes(factors.at[sc, g], fx_s.at[sc, d, k])
            for k in ((0, 3), (1, 2))[d]:
                await_bytes(factors.at[sc, g], ff_s.at[sc, d, k])
            for n in range(2):
                await_bytes(x_part(sc, 0, d), sx_s.at[sc, d, n])
                await_bytes(x_part(sc, 0, d, 0, SB // 2), sx_s.at[sc, d, 2 + n])
    for k in range(NZ - 1):

        @pl.when((z - k >= 0) & (z < NZ - 1))
        def _(k=k):
            for h in range(2):
                await_bytes(z_half(raw_z.at[0], h), zl_s.at[0, k, h])

        @pl.when((z + k <= NZ - 1) & (z > 0))
        def _(k=k):
            for h in range(2):
                await_bytes(z_half(raw_z.at[0], h), zl_s.at[1, k, h])

    for batch in range(3):
        await_bytes(from_core.at[span(batch)], c_s.at[batch])
    for batch in range(3):
        for k in range(NY - 1):
            await_bytes(from_y.at[k, span(batch)], y_s.at[batch, k])
    for batch in range(3):
        for o in OTHERS[batch]:
            await_bytes(batch_z(near_z, 0, batch), nz_s.at[batch, o])
        for i in WIDTH[batch]:
            if i:
                await_bytes(batch_x(near_x, 0, batch), nx_s.at[batch, i - 1])
    await_bytes(final, fn_r.at[0])

    @pl.when(z > s % NZ)
    def _():
        out[...] = ((final[0].astype(F32) + final[1].astype(F32)) * scaling).T

    @pl.when(z <= s % NZ)
    def _():
        out[...] = (final[0].astype(F32) + final[1].astype(F32)) * scaling

    for o in range(4):
        for i in range(4):

            @pl.when(at_x(i) * NZ + places[o] != s)
            def _(o=o, i=i):
                await_bytes(slices.at[0, 0], fn_s.at[o * 4 + i])


def local(linking, reach_count, diag_inverse, off_blocks, targets):
    scaling = 1.0 / math.sqrt(linking.shape[0] * 16 * ROWS)
    dma = pltpu.SemaphoreType.DMA
    vmem = pl.BlockSpec(memory_space=pltpu.VMEM)
    hbm = pl.BlockSpec(memory_space=pltpu.HBM)

    def body(*refs):
        kernel(scaling, *refs)

    operands = (jnp.swapaxes(targets, 1, 2), reach_count, linking, diag_inverse, off_blocks)
    return pl.pallas_call(
        body,
        out_shape=jax.ShapeDtypeStruct((SB, SB), F32),
        in_specs=[hbm] * 5,
        out_specs=vmem,
        scratch_shapes=[
            pltpu.SMEM((2, 2, NS), jnp.int32),
            pltpu.SMEM((2,), jnp.int32),
            pltpu.VMEM((2, ROWS, SB), BF16),
            pltpu.VMEM((2, 2, 16, SB), BF16),
            pltpu.VMEM((2, 16, PACK, 16, SB), BF16),
            pltpu.VMEM((2, NS - 1, SB, 3 * SB), BF16),
            pltpu.VMEM((2, SB, ROWS), BF16),
            pltpu.VMEM((2, NX, SB, ROWS), BF16),
            pltpu.VMEM((NZ, SB, ROWS), BF16),
            pltpu.VMEM((NZ, SB, ROWS), BF16),
            pltpu.VMEM((2, TILES, SB // 2, SB), F32),
            pltpu.VMEM((TILES, SB // 2, SB), F32),
            pltpu.VMEM((NY - 1, TILES, 32, SB), BF16),
            pltpu.VMEM((NY - 1, TILES, 32, SB), BF16),
            pltpu.VMEM((3, NX, 32, SB), BF16),
            pltpu.VMEM((NZ, NX, 32, SB), BF16),
            pltpu.VMEM((NX, 3, 32, SB), BF16),
            pltpu.VMEM((4, NX, 32, SB), BF16),
            pltpu.VMEM((2, SB, SB), BF16),
            dma((11,)),
            dma((2, 5)),
            dma((2, 4)),
            dma((2, 2, 4)),
            dma((2, 2, 4)),
            dma((2, 2, 4)),
            dma((2, 2, 4)),
            dma((2, 2, 4)),
            dma((2, 2, 4)),
            dma((2, 3, 2)),
            dma((2, 3, 2)),
            dma((3,)),
            dma((3,)),
            dma((3, 3)),
            dma((3, 3)),
            dma((3, 3)),
            dma((3, 4)),
            dma((3, 3)),
            dma((3, 3)),
            dma((16,)),
            dma((1,)),
        ],
        compiler_params=pltpu.CompilerParams(
            collective_id=0,
            has_side_effects=True,
            vmem_limit_bytes=44 * 1024 * 1024,
        ),
        cost_estimate=pl.CostEstimate(flops=3_000_000_000, bytes_accessed=5_000_000, transcendentals=0),
    )(*(pltpu.with_memory_space_constraint(a, pltpu.HBM) for a in operands))


def solution(mesh):
    return jax.shard_map(
        local,
        mesh=mesh,
        in_specs=(
            P("scen", None, "grp"),
            P("scen"),
            P("scen", None, "grp", None),
            P("scen", None, None, "grp", None),
            P("scen", None, None),
        ),
        out_specs=P("grp", "scen"),
        check_vma=False,
    )
```

```python
import math

import jax
import jax.numpy as jnp
from jax import lax
from jax.experimental import pallas as pl
from jax.experimental.pallas import tpu as pltpu
from jax.sharding import PartitionSpec as P

F32 = jnp.float32
BF16 = jnp.bfloat16
MESH = pl.DeviceIdType.MESH

NX = 4
NZ = 4
NY = 4
SB = 256
NS = 4
ROWS = NS * SB
HALF = ROWS // 2
PACK = 9
REL = (0, 1, 3, 2)

BATCHES = (
    ((3, 0), (3, 1), (3, 2), (0, 0), (0, 1), (0, 2)),
    ((1, 0), (1, 1), (1, 2), (2, 0), (2, 1), (2, 2)),
    ((3, 3), (0, 3), (1, 3), (2, 3)),
)
STARTS = (0, 6, 12)
OTHERS = ((0,), (1, 2), (0, 1, 2))
WIDTH = ((0, 1, 2), (0, 1, 2), (3,))
TILES = 16


def send(src, dst, send_sem, recv_sem, device):
    pltpu.make_async_remote_copy(
        src_ref=src,
        dst_ref=dst,
        send_sem=send_sem,
        recv_sem=recv_sem,
        device_id=device,
        device_id_type=MESH,
    ).start()


def await_bytes(ref, sem):
    pltpu.make_async_copy(ref, ref, sem).wait()


def flag(condition):
    return jnp.where(condition, 1.0, 0.0).astype(F32)


def mm(a, b):
    return lax.dot_general(a, b, (((1,), (1,)), ((), ())), preferred_element_type=F32)


def kernel(
    scaling,
    targets_hbm,
    reach_hbm,
    linking_hbm,
    diag,
    off,
    out,
    targets,
    reach,
    linking,
    choice,
    factors,
    lower,
    columns,
    solved,
    raw_z,
    solved_z,
    partial,
    from_core,
    to_y,
    from_y,
    reduced,
    near_z,
    near_x,
    slices,
    final,
    in_s,
    fz_s,
    fz_r,
    fx_s,
    fx_r,
    ff_s,
    ff_r,
    sx_s,
    sx_r,
    zl_s,
    zl_r,
    c_s,
    c_r,
    y_s,
    y_r,
    nz_s,
    nz_r,
    nx_s,
    nx_r,
    fn_s,
    fn_r,
):
    s = lax.axis_index("scen")
    g = lax.axis_index("grp")
    x, z = g // NZ, g % NZ
    core, y, z_hi = s % 2, (s // 2) % NY, s // (2 * NY)
    right_x, left_x, far_x = (x + 1) % NX, (x + 3) % NX, (x + 2) % NX
    right = (s, right_x * NZ + z)
    left = (s, left_x * NZ + z)
    upper = z // 2
    places = (z + 1 - 2 * (z % 2), 2 - upper, 3 - 3 * upper, z)

    def at_x(i):
        return (x + REL[i]) % NX

    barrier = pltpu.get_barrier_semaphore()

    def greet(k, carry):
        pl.semaphore_signal(barrier, inc=1, device_id=((s + k) % 16, g), device_id_type=MESH)
        return carry

    lax.fori_loop(1, 16, greet, 0)
    for k in range(1, NZ):
        pl.semaphore_signal(barrier, inc=1, device_id=(s, x * NZ + (z + k) % NZ), device_id_type=MESH)
    for k in range(1, NX):
        pl.semaphore_signal(barrier, inc=1, device_id=(s, ((x + k) % NX) * NZ + z), device_id_type=MESH)

    fetches = [(targets_hbm, targets), (reach_hbm, reach)]
    for sc in range(2):
        fetches.append((off.at[sc, 2], choice.at[sc]))
        fetches.append((diag.at[sc], factors.at[sc, g, pl.ds(0, NS)]))
        for i in range(2):
            fetches.append((off.at[sc, i], factors.at[sc, g, pl.ds(NS + 2 * i, 2)]))
    fetches.append((linking_hbm, linking))
    copies = [pltpu.make_async_copy(a, b, in_s.at[n]) for n, (a, b) in enumerate(fetches)]
    for copy in copies:
        copy.start()
    for copy in copies[:-1]:
        copy.wait()
    for sc in range(2):
        first = choice[sc, 0].astype(F32) * flag(targets[sc, 0, 2] == 3)
        second = choice[sc, 1].astype(F32) * flag(targets[sc, 1, 2] == 3)
        factors[sc, g, 8] = (first + second).astype(BF16)

    pl.semaphore_wait(barrier, 21)

    def shard(sc, xx, k):
        return factors.at[sc, xx * NZ + (z + k) % NZ]

    def x_send(sc, k):
        piece = shard(sc, x, k)
        send(piece, piece, fx_s.at[sc, 0, k], fx_r.at[sc, 0, k], right)
        send(piece, piece, fx_s.at[sc, 1, k], fx_r.at[sc, 1, k], left)

    def goes_on(q):
        return ((q < z) & (z < NZ - 1), (q > z) & (z > 0))

    def z_take(sc, o):
        q = places[o]
        piece = factors.at[sc, x * NZ + q]
        await_bytes(piece, fz_r.at[sc, q])
        for onward, device in zip(goes_on(q), ((s, g + 1), (s, g - 1))):

            @pl.when(onward)
            def _(device=device):
                send(piece, piece, fz_s.at[sc, 2 + o], fz_r.at[sc, q], device)

        x_send(sc, (q + NZ - z) % NZ)

    def pass_right(sc, k):
        piece = shard(sc, left_x, k)
        await_bytes(piece, fx_r.at[sc, 0, k])
        send(piece, piece, ff_s.at[sc, 0, k], ff_r.at[sc, 0, k], right)

    def pass_left(sc, k):
        piece = shard(sc, right_x, k)
        await_bytes(piece, fx_r.at[sc, 1, k])
        send(piece, piece, ff_s.at[sc, 1, k], ff_r.at[sc, 1, k], left)

    def rest(sc):
        for k in (1, 2):
            await_bytes(shard(sc, left_x, k), fx_r.at[sc, 0, k])
            await_bytes(shard(sc, far_x, k), ff_r.at[sc, 1, k])
        for k in (0, 3):
            await_bytes(shard(sc, right_x, k), fx_r.at[sc, 1, k])
            await_bytes(shard(sc, far_x, k), ff_r.at[sc, 0, k])

    def z_send(sc):
        own = factors.at[sc, g]

        @pl.when(z < NZ - 1)
        def _():
            send(own, own, fz_s.at[sc, 0], fz_r.at[sc, z], (s, g + 1))

        @pl.when(z > 0)
        def _():
            send(own, own, fz_s.at[sc, 1], fz_r.at[sc, z], (s, g - 1))

        x_send(sc, 0)

    def prepare(sc):
        for i in range(3):
            for j in range(i + 1, NS):
                if i == 2:
                    block = factors[sc, :, 8].reshape(SB, SB)
                else:
                    block = jnp.zeros((SB, SB), BF16)
                    for p in range(2):
                        chosen = flag(targets[sc, p, i] == j).astype(BF16)
                        block = block + factors[sc, :, 4 + 2 * i + p].reshape(SB, SB) * chosen
                lower[sc, j - 1, :, i * SB : (i + 1) * SB] = block

    def solve(sc, source, target, own=False, after=None):
        for j in range(NS):
            if own and j == 1:
                prepare(sc)
            here = slice(j * SB, (j + 1) * SB)
            residual = source[:, here].astype(F32) * flag(j >= NS - reach[sc])
            if j:
                residual = residual - mm(target[:, : j * SB], lower[sc, j - 1, :, : j * SB])
            inverse = factors[sc, :, j].reshape(SB, SB)
            target[:, here] = mm(residual.astype(BF16), inverse).astype(BF16)
            if after is not None:
                after(j)

    def x_part(sc, i, form, first=0, count=SB):
        return solved.at[sc, i, pl.ds(first, count), pl.ds(form * HALF, HALF)]

    def solve_own(sc):
        def after(j):
            if j % 2:
                form = j // 2
                own = x_part(sc, 0, form)
                send(own, x_part(sc, 2, form), sx_s.at[sc, form, 0], sx_r.at[sc, form, 0], right)
                send(own, x_part(sc, 1, form), sx_s.at[sc, form, 1], sx_r.at[sc, form, 1], left)

        solve(sc, columns.at[sc], solved.at[sc, 0], True, after)

    def pass_x(sc, form):
        await_bytes(x_part(sc, 2, form), sx_r.at[sc, form, 0])
        send(
            x_part(sc, 2, form, 0, SB // 2),
            x_part(sc, 3, form, 0, SB // 2),
            sx_s.at[sc, form, 2],
            sx_r.at[sc, form, 2],
            right,
        )
        await_bytes(x_part(sc, 1, form), sx_r.at[sc, form, 1])
        send(
            x_part(sc, 1, form, SB // 2, SB // 2),
            x_part(sc, 3, form, SB // 2, SB // 2),
            sx_s.at[sc, form, 3],
            sx_r.at[sc, form, 3],
            left,
        )

    def far(sc, form):
        for n in range(2):
            await_bytes(x_part(sc, 3, form, n * (SB // 2), SB // 2), sx_r.at[sc, form, 2 + n])

    def z_half(ref, h):
        return ref.at[pl.ds(h * (SB // 2), SB // 2)]

    def start_z():
        for h in range(2):

            @pl.when(z < NZ - 1)
            def _(h=h):
                send(z_half(columns.at[0], h), z_half(raw_z.at[z], h), zl_s.at[0, 0, h], zl_r.at[0, 0, h], (s, g + 1))

            @pl.when(z > 0)
            def _(h=h):
                send(z_half(columns.at[1], h), z_half(raw_z.at[z], h), zl_s.at[1, 0, h], zl_r.at[1, 0, h], (s, g - 1))

    def pass_z(k):
        for h in range(2):

            @pl.when(z - k >= 0)
            def _(h=h):
                block = z_half(raw_z.at[z - k], h)
                await_bytes(block, zl_r.at[0, k - 1, h])
                if k < NZ - 1:

                    @pl.when(z < NZ - 1)
                    def _():
                        send(block, block, zl_s.at[0, k, h], zl_r.at[0, k, h], (s, g + 1))

            @pl.when(z + k <= NZ - 1)
            def _(h=h):
                block = z_half(raw_z.at[z + k], h)
                await_bytes(block, zl_r.at[1, k - 1, h])
                if k < NZ - 1:

                    @pl.when(z > 0)
                    def _():
                        send(block, block, zl_s.at[1, k, h], zl_r.at[1, k, h], (s, g - 1))

    def solve_z(o):
        sc = (1 - z % 2) if o == 0 else (1 - upper)
        solve(sc, raw_z.at[places[o]], solved_z.at[places[o]])

    z_send(0)
    z_send(1)
    copies[-1].wait()
    for sc in range(2):
        for j in range(NS):
            block = linking[sc, j * SB : (j + 1) * SB, :].astype(F32)
            columns[sc, :, j * SB : (j + 1) * SB] = block.T.astype(BF16)
    z_take(0, 0)
    z_take(0, 1)
    z_take(1, 0)
    z_take(1, 1)
    pass_right(0, 0)
    z_take(0, 2)
    z_take(1, 2)
    start_z()
    pass_left(0, 1)
    pass_left(0, 2)
    pass_right(0, 3)
    pass_right(1, 3)
    pass_left(1, 1)
    pass_right(1, 0)
    pass_left(1, 2)
    rest(0)
    solve_own(0)
    pass_z(1)
    rest(1)
    solve_own(1)

    def store(n, tile):
        partial[0, n] = tile[: SB // 2]
        partial[1, n] = tile[SB // 2 :]

    def wide(sc):
        return solved[sc, 0:3].reshape(3 * SB, ROWS)

    def store_wide(n, product, axis):
        for i in range(3):
            store(n + i, lax.slice_in_dim(product, i * SB, (i + 1) * SB, axis=axis))

    def pair(first):
        return solved_z[first : first + 2].reshape(2 * SB, ROWS)

    def gram(batch):
        near_below = z % 2 == 1
        below = upper == 1
        if batch == 0:
            store_wide(0, mm(solved[0, 0], wide(0)) + mm(solved[1, 0], wide(1)), 1)

            @pl.when(near_below)
            def _():
                store_wide(3, mm(solved_z[places[0]], wide(0)), 1)

            @pl.when(jnp.logical_not(near_below))
            def _():
                store_wide(3, mm(wide(1), solved_z[places[0]]), 0)
        elif batch == 1:
            @pl.when(below)
            def _():
                product = mm(pair(0), wide(0))
                store_wide(6, product[SB:], 1)
                store_wide(9, product[:SB], 1)

            @pl.when(jnp.logical_not(below))
            def _():
                product = mm(wide(1), pair(2))
                store_wide(6, product[:, :SB], 0)
                store_wide(9, product[:, SB:], 0)
        else:
            store(12, mm(solved[0, 0], solved[0, 3]) + mm(solved[1, 0], solved[1, 3]))

            @pl.when(near_below)
            def _():
                store(13, mm(solved_z[places[0]], solved[0, 3]))

            @pl.when(jnp.logical_not(near_below))
            def _():
                store(13, mm(solved[1, 3], solved_z[places[0]]))

            @pl.when(below)
            def _():
                product = mm(pair(0), solved[0, 3])
                store(14, product[SB:])
                store(15, product[:SB])

            @pl.when(jnp.logical_not(below))
            def _():
                product = mm(solved[1, 3], pair(2))
                store(14, product[:, :SB])
                store(15, product[:, SB:])

    def span(batch):
        return pl.ds(STARTS[batch], len(BATCHES[batch]))

    def to_core(batch):
        send(
            partial.at[1 - core, span(batch)],
            from_core.at[span(batch)],
            c_s.at[batch],
            c_r.at[batch],
            (s + 1 - 2 * core, g),
        )

    def of_y(yy, first=0, count=32):
        return pl.ds(pl.multiple_of((yy % NY) * 32 + first, 16), count)

    def both_cores(n, rows):
        return partial[core, n, rows, :] + from_core[n, rows, :]

    def over_tiles(batch, body):
        def step(n, carry):
            body(n)
            return carry

        lax.fori_loop(STARTS[batch], STARTS[batch] + len(BATCHES[batch]), step, 0)

    def along_y(batch):
        tiles = span(batch)
        await_bytes(from_core.at[tiles], c_r.at[batch])
        for k in (2, 1, 3):

            def body(n, k=k):
                to_y[k - 1, n] = both_cores(n, of_y(y + k)).astype(BF16)

            over_tiles(batch, body)
            send(
                to_y.at[k - 1, tiles],
                from_y.at[k - 1, tiles],
                y_s.at[batch, k - 1],
                y_r.at[batch, k - 1],
                (z_hi * 8 + ((y + k) % NY) * 2 + core, g),
            )

    def finish_y(batch):
        tiles = span(batch)
        for k in range(1, NY):
            await_bytes(from_y.at[k - 1, tiles], y_r.at[batch, k - 1])
        for n, (o, i) in enumerate(BATCHES[batch], STARTS[batch]):
            value = both_cores(n, of_y(y))
            for k in range(1, NY):
                value += from_y[k - 1, n].astype(F32)
            value = value.astype(BF16)
            if o == 3:
                slices[3, i] = value
            else:
                reduced[o, i] = value
                if i == 0:
                    near_x[0, o] = value

    def batch_z(ref, place, batch):
        return ref.at[place, pl.ds(WIDTH[batch][0], len(WIDTH[batch]))]

    def batch_x(ref, place, batch):
        return ref.at[place, pl.ds(OTHERS[batch][0], len(OTHERS[batch]))]

    def to_groups(batch):
        for o in OTHERS[batch]:
            send(
                batch_z(reduced, o, batch),
                batch_z(near_z, z, batch),
                nz_s.at[batch, o],
                nz_r.at[batch, z],
                (s, x * NZ + places[o]),
            )
        for i in WIDTH[batch]:
            if i:
                back = (0, 2, 1, 3)[i]
                send(
                    reduced.at[pl.ds(OTHERS[batch][0], len(OTHERS[batch])), i],
                    batch_x(near_x, back, batch),
                    nx_s.at[batch, i - 1],
                    nx_r.at[batch, back - 1],
                    (s, at_x(i) * NZ + z),
                )

    def from_groups(batch):
        for o in OTHERS[batch]:
            await_bytes(batch_z(near_z, places[o], batch), nz_r.at[batch, places[o]])
        for i in WIDTH[batch]:
            if i:
                await_bytes(batch_x(near_x, i, batch), nx_r.at[batch, i - 1])
        for o in OTHERS[batch]:
            for i in WIDTH[batch]:
                deliver(o, i)

    out_rows = pl.ds(pl.multiple_of(core * 128 + y * 32, 32), 32)

    def deliver(o, i):
        if o < 3:
            both = near_z[places[o], i].astype(F32) + near_x[i, o].astype(F32)
            slices[o, i] = both.astype(BF16)
        b = at_x(i) * NZ + places[o]
        piece = slices.at[o, i]
        target = final.at[z_hi, out_rows]

        @pl.when(b == s)
        def _():
            pltpu.make_async_copy(piece, target, fn_r.at[0]).start()

        @pl.when(b != s)
        def _():
            send(piece, target, fn_s.at[o * 4 + i], fn_r.at[0], (b, g))

    pass_z(2)
    solve_z(0)
    pass_x(0, 0)
    solve_z(1)
    pass_x(0, 1)
    pass_x(1, 0)
    pass_x(1, 1)
    gram(0)
    to_core(0)
    pass_z(3)
    solve_z(2)
    along_y(0)
    gram(1)
    to_core(1)
    far(0, 0)
    far(0, 1)
    along_y(1)
    far(1, 0)
    far(1, 1)
    gram(2)
    to_core(2)
    finish_y(0)
    to_groups(0)
    for i in range(3):
        deliver(3, i)
    along_y(2)
    from_groups(0)
    finish_y(1)
    to_groups(1)
    finish_y(2)
    to_groups(2)
    from_groups(1)
    deliver(3, 3)
    from_groups(2)

    for sc in range(2):

        @pl.when(z < NZ - 1)
        def _(sc=sc):
            await_bytes(factors.at[sc, g], fz_s.at[sc, 0])

        @pl.when(z > 0)
        def _(sc=sc):
            await_bytes(factors.at[sc, g], fz_s.at[sc, 1])

        for o in range(3):
            for onward in goes_on(places[o]):

                @pl.when(onward)
                def _(sc=sc, o=o):
                    await_bytes(factors.at[sc, g], fz_s.at[sc, 2 + o])

        for d in range(2):
            for k in range(4):
                await_bytes(factors.at[sc, g], fx_s.at[sc, d, k])
            for k in ((0, 3), (1, 2))[d]:
                await_bytes(factors.at[sc, g], ff_s.at[sc, d, k])
            for n in range(2):
                await_bytes(x_part(sc, 0, d), sx_s.at[sc, d, n])
                await_bytes(x_part(sc, 0, d, 0, SB // 2), sx_s.at[sc, d, 2 + n])
    for k in range(NZ - 1):

        @pl.when((z - k >= 0) & (z < NZ - 1))
        def _(k=k):
            for h in range(2):
                await_bytes(z_half(raw_z.at[0], h), zl_s.at[0, k, h])

        @pl.when((z + k <= NZ - 1) & (z > 0))
        def _(k=k):
            for h in range(2):
                await_bytes(z_half(raw_z.at[0], h), zl_s.at[1, k, h])

    for batch in range(3):
        await_bytes(from_core.at[span(batch)], c_s.at[batch])
    for batch in range(3):
        for k in range(NY - 1):
            await_bytes(from_y.at[k, span(batch)], y_s.at[batch, k])
    for batch in range(3):
        for o in OTHERS[batch]:
            await_bytes(batch_z(near_z, 0, batch), nz_s.at[batch, o])
        for i in WIDTH[batch]:
            if i:
                await_bytes(batch_x(near_x, 0, batch), nx_s.at[batch, i - 1])
    await_bytes(final, fn_r.at[0])

    @pl.when(z > s % NZ)
    def _():
        out[...] = ((final[0].astype(F32) + final[1].astype(F32)) * scaling).T

    @pl.when(z <= s % NZ)
    def _():
        out[...] = (final[0].astype(F32) + final[1].astype(F32)) * scaling

    for o in range(4):
        for i in range(4):

            @pl.when(at_x(i) * NZ + places[o] != s)
            def _(o=o, i=i):
                await_bytes(slices.at[0, 0], fn_s.at[o * 4 + i])


def local(linking, reach_count, diag_inverse, off_blocks, targets):
    scaling = 1.0 / math.sqrt(linking.shape[0] * 16 * ROWS)
    dma = pltpu.SemaphoreType.DMA
    vmem = pl.BlockSpec(memory_space=pltpu.VMEM)
    hbm = pl.BlockSpec(memory_space=pltpu.HBM)

    def body(*refs):
        kernel(scaling, *refs)

    operands = (jnp.swapaxes(targets, 1, 2), reach_count, linking, diag_inverse, off_blocks)
    return pl.pallas_call(
        body,
        out_shape=jax.ShapeDtypeStruct((SB, SB), F32),
        in_specs=[hbm] * 5,
        out_specs=vmem,
        scratch_shapes=[
            pltpu.SMEM((2, 2, NS), jnp.int32),
            pltpu.SMEM((2,), jnp.int32),
            pltpu.VMEM((2, ROWS, SB), BF16),
            pltpu.VMEM((2, 2, 16, SB), BF16),
            pltpu.VMEM((2, 16, PACK, 16, SB), BF16),
            pltpu.VMEM((2, NS - 1, SB, 3 * SB), BF16),
            pltpu.VMEM((2, SB, ROWS), BF16),
            pltpu.VMEM((2, NX, SB, ROWS), BF16),
            pltpu.VMEM((NZ, SB, ROWS), BF16),
            pltpu.VMEM((NZ, SB, ROWS), BF16),
            pltpu.VMEM((2, TILES, SB // 2, SB), F32),
            pltpu.VMEM((TILES, SB // 2, SB), F32),
            pltpu.VMEM((NY - 1, TILES, 32, SB), BF16),
            pltpu.VMEM((NY - 1, TILES, 32, SB), BF16),
            pltpu.VMEM((3, NX, 32, SB), BF16),
            pltpu.VMEM((NZ, NX, 32, SB), BF16),
            pltpu.VMEM((NX, 3, 32, SB), BF16),
            pltpu.VMEM((4, NX, 32, SB), BF16),
            pltpu.VMEM((2, SB, SB), BF16),
            dma((11,)),
            dma((2, 5)),
            dma((2, 4)),
            dma((2, 2, 4)),
            dma((2, 2, 4)),
            dma((2, 2, 4)),
            dma((2, 2, 4)),
            dma((2, 2, 4)),
            dma((2, 2, 4)),
            dma((2, 3, 2)),
            dma((2, 3, 2)),
            dma((3,)),
            dma((3,)),
            dma((3, 3)),
            dma((3, 3)),
            dma((3, 3)),
            dma((3, 4)),
            dma((3, 3)),
            dma((3, 3)),
            dma((16,)),
            dma((1,)),
        ],
        compiler_params=pltpu.CompilerParams(
            collective_id=0,
            has_side_effects=True,
            vmem_limit_bytes=44 * 1024 * 1024,
        ),
        cost_estimate=pl.CostEstimate(flops=3_000_000_000, bytes_accessed=5_000_000, transcendentals=0),
    )(*(pltpu.with_memory_space_constraint(a, pltpu.HBM) for a in operands))


def solution(mesh):
    return jax.shard_map(
        local,
        mesh=mesh,
        in_specs=(
            P("scen", None, "grp"),
            P("scen"),
            P("scen", None, "grp", None),
            P("scen", None, None, "grp", None),
            P("scen", None, None),
        ),
        out_specs=P("grp", "scen"),
        check_vma=False,
    )
```

```python
import math

import jax
import jax.numpy as jnp
from jax import lax
from jax.experimental import pallas as pl
from jax.experimental.pallas import tpu as pltpu
from jax.sharding import PartitionSpec as P

F32 = jnp.float32
BF16 = jnp.bfloat16
MESH = pl.DeviceIdType.MESH

NX = 4
NZ = 4
NY = 4
SB = 256
NS = 4
ROWS = NS * SB
HALF = ROWS // 2
PACK = 9
REL = (0, 1, 3, 2)

BATCHES = (
    ((3, 0), (3, 1), (3, 2), (0, 0), (0, 1), (0, 2)),
    ((1, 0), (1, 1), (1, 2), (2, 0), (2, 1), (2, 2)),
    ((3, 3), (0, 3), (1, 3), (2, 3)),
)
STARTS = (0, 6, 12)
OTHERS = ((0,), (1, 2), (0, 1, 2))
WIDTH = ((0, 1, 2), (0, 1, 2), (3,))
TILES = 16


def send(src, dst, send_sem, recv_sem, device):
    pltpu.make_async_remote_copy(
        src_ref=src,
        dst_ref=dst,
        send_sem=send_sem,
        recv_sem=recv_sem,
        device_id=device,
        device_id_type=MESH,
    ).start()


def await_bytes(ref, sem):
    pltpu.make_async_copy(ref, ref, sem).wait()


def flag(condition):
    return jnp.where(condition, 1.0, 0.0).astype(F32)


def mm(a, b):
    return lax.dot_general(a, b, (((1,), (1,)), ((), ())), preferred_element_type=F32)


def kernel(
    scaling,
    targets_hbm,
    reach_hbm,
    linking_hbm,
    diag,
    off,
    out,
    targets,
    reach,
    linking,
    choice,
    factors,
    lower,
    columns,
    solved,
    raw_z,
    solved_z,
    partial,
    from_core,
    to_y,
    from_y,
    reduced,
    near_z,
    near_x,
    slices,
    final,
    in_s,
    fz_s,
    fz_r,
    fx_s,
    fx_r,
    ff_s,
    ff_r,
    sx_s,
    sx_r,
    zl_s,
    zl_r,
    c_s,
    c_r,
    y_s,
    y_r,
    nz_s,
    nz_r,
    nx_s,
    nx_r,
    fn_s,
    fn_r,
):
    s = lax.axis_index("scen")
    g = lax.axis_index("grp")
    x, z = g // NZ, g % NZ
    core, y, z_hi = s % 2, (s // 2) % NY, s // (2 * NY)
    right_x, left_x, far_x = (x + 1) % NX, (x + 3) % NX, (x + 2) % NX
    right = (s, right_x * NZ + z)
    left = (s, left_x * NZ + z)
    upper = z // 2
    places = (z + 1 - 2 * (z % 2), 2 - upper, 3 - 3 * upper, z)

    def at_x(i):
        return (x + REL[i]) % NX

    barrier = pltpu.get_barrier_semaphore()

    def greet(k, carry):
        pl.semaphore_signal(barrier, inc=1, device_id=((s + k) % 16, g), device_id_type=MESH)
        return carry

    lax.fori_loop(1, 16, greet, 0)
    for k in range(1, NZ):
        pl.semaphore_signal(barrier, inc=1, device_id=(s, x * NZ + (z + k) % NZ), device_id_type=MESH)
    for k in range(1, NX):
        pl.semaphore_signal(barrier, inc=1, device_id=(s, ((x + k) % NX) * NZ + z), device_id_type=MESH)

    fetches = [(targets_hbm, targets), (reach_hbm, reach)]
    for sc in range(2):
        fetches.append((off.at[sc, 2], choice.at[sc]))
        fetches.append((diag.at[sc], factors.at[sc, g, pl.ds(0, NS)]))
        for i in range(2):
            fetches.append((off.at[sc, i], factors.at[sc, g, pl.ds(NS + 2 * i, 2)]))
    fetches.append((linking_hbm, linking))
    copies = [pltpu.make_async_copy(a, b, in_s.at[n]) for n, (a, b) in enumerate(fetches)]
    for copy in copies:
        copy.start()
    for copy in copies[:-1]:
        copy.wait()
    for sc in range(2):
        first = choice[sc, 0].astype(F32) * flag(targets[sc, 0, 2] == 3)
        second = choice[sc, 1].astype(F32) * flag(targets[sc, 1, 2] == 3)
        factors[sc, g, 8] = (first + second).astype(BF16)

    pl.semaphore_wait(barrier, 21)

    def shard(sc, xx, k):
        return factors.at[sc, xx * NZ + (z + k) % NZ]

    def x_send(sc, k):
        piece = shard(sc, x, k)
        send(piece, piece, fx_s.at[sc, 0, k], fx_r.at[sc, 0, k], right)
        send(piece, piece, fx_s.at[sc, 1, k], fx_r.at[sc, 1, k], left)

    def goes_on(q):
        return ((q < z) & (z < NZ - 1), (q > z) & (z > 0))

    def z_take(sc, o):
        q = places[o]
        piece = factors.at[sc, x * NZ + q]
        await_bytes(piece, fz_r.at[sc, q])
        for onward, device in zip(goes_on(q), ((s, g + 1), (s, g - 1))):

            @pl.when(onward)
            def _(device=device):
                send(piece, piece, fz_s.at[sc, 2 + o], fz_r.at[sc, q], device)

        x_send(sc, (q + NZ - z) % NZ)

    def pass_right(sc, k):
        piece = shard(sc, left_x, k)
        await_bytes(piece, fx_r.at[sc, 0, k])
        send(piece, piece, ff_s.at[sc, 0, k], ff_r.at[sc, 0, k], right)

    def pass_left(sc, k):
        piece = shard(sc, right_x, k)
        await_bytes(piece, fx_r.at[sc, 1, k])
        send(piece, piece, ff_s.at[sc, 1, k], ff_r.at[sc, 1, k], left)

    def rest(sc):
        for k in (1, 2):
            await_bytes(shard(sc, left_x, k), fx_r.at[sc, 0, k])
            await_bytes(shard(sc, far_x, k), ff_r.at[sc, 1, k])
        for k in (0, 3):
            await_bytes(shard(sc, right_x, k), fx_r.at[sc, 1, k])
            await_bytes(shard(sc, far_x, k), ff_r.at[sc, 0, k])

    def z_send(sc):
        own = factors.at[sc, g]

        @pl.when(z < NZ - 1)
        def _():
            send(own, own, fz_s.at[sc, 0], fz_r.at[sc, z], (s, g + 1))

        @pl.when(z > 0)
        def _():
            send(own, own, fz_s.at[sc, 1], fz_r.at[sc, z], (s, g - 1))

        x_send(sc, 0)

    def prepare(sc):
        for i in range(3):
            for j in range(i + 1, NS):
                if i == 2:
                    block = factors[sc, :, 8].reshape(SB, SB)
                else:
                    block = jnp.zeros((SB, SB), BF16)
                    for p in range(2):
                        chosen = flag(targets[sc, p, i] == j).astype(BF16)
                        block = block + factors[sc, :, 4 + 2 * i + p].reshape(SB, SB) * chosen
                lower[sc, j - 1, :, i * SB : (i + 1) * SB] = block

    def solve(sc, source, target, own=False, after=None):
        for j in range(NS):
            if own and j == 1:
                prepare(sc)
            here = slice(j * SB, (j + 1) * SB)
            residual = source[:, here].astype(F32) * flag(j >= NS - reach[sc])
            if j:
                residual = residual - mm(target[:, : j * SB], lower[sc, j - 1, :, : j * SB])
            inverse = factors[sc, :, j].reshape(SB, SB)
            target[:, here] = mm(residual.astype(BF16), inverse).astype(BF16)
            if after is not None:
                after(j)

    def x_part(sc, i, form, first=0, count=SB):
        return solved.at[sc, i, pl.ds(first, count), pl.ds(form * HALF, HALF)]

    def solve_own(sc):
        def after(j):
            if j % 2:
                form = j // 2
                own = x_part(sc, 0, form)
                send(own, x_part(sc, 2, form), sx_s.at[sc, form, 0], sx_r.at[sc, form, 0], right)
                send(own, x_part(sc, 1, form), sx_s.at[sc, form, 1], sx_r.at[sc, form, 1], left)

        solve(sc, columns.at[sc], solved.at[sc, 0], True, after)

    def pass_x(sc, form):
        await_bytes(x_part(sc, 2, form), sx_r.at[sc, form, 0])
        send(
            x_part(sc, 2, form, 0, SB // 2),
            x_part(sc, 3, form, 0, SB // 2),
            sx_s.at[sc, form, 2],
            sx_r.at[sc, form, 2],
            right,
        )
        await_bytes(x_part(sc, 1, form), sx_r.at[sc, form, 1])
        send(
            x_part(sc, 1, form, SB // 2, SB // 2),
            x_part(sc, 3, form, SB // 2, SB // 2),
            sx_s.at[sc, form, 3],
            sx_r.at[sc, form, 3],
            left,
        )

    def far(sc, form):
        for n in range(2):
            await_bytes(x_part(sc, 3, form, n * (SB // 2), SB // 2), sx_r.at[sc, form, 2 + n])

    def z_half(ref, h):
        return ref.at[pl.ds(h * (SB // 2), SB // 2)]

    def start_z():
        for h in range(2):

            @pl.when(z < NZ - 1)
            def _(h=h):
                send(z_half(columns.at[0], h), z_half(raw_z.at[z], h), zl_s.at[0, 0, h], zl_r.at[0, 0, h], (s, g + 1))

            @pl.when(z > 0)
            def _(h=h):
                send(z_half(columns.at[1], h), z_half(raw_z.at[z], h), zl_s.at[1, 0, h], zl_r.at[1, 0, h], (s, g - 1))

    def pass_z(k):
        for h in range(2):

            @pl.when(z - k >= 0)
            def _(h=h):
                block = z_half(raw_z.at[z - k], h)
                await_bytes(block, zl_r.at[0, k - 1, h])
                if k < NZ - 1:

                    @pl.when(z < NZ - 1)
                    def _():
                        send(block, block, zl_s.at[0, k, h], zl_r.at[0, k, h], (s, g + 1))

            @pl.when(z + k <= NZ - 1)
            def _(h=h):
                block = z_half(raw_z.at[z + k], h)
                await_bytes(block, zl_r.at[1, k - 1, h])
                if k < NZ - 1:

                    @pl.when(z > 0)
                    def _():
                        send(block, block, zl_s.at[1, k, h], zl_r.at[1, k, h], (s, g - 1))

    def solve_z(o):
        sc = (1 - z % 2) if o == 0 else (1 - upper)
        solve(sc, raw_z.at[places[o]], solved_z.at[places[o]])

    z_send(0)
    z_send(1)
    copies[-1].wait()
    for sc in range(2):
        for j in range(NS):
            block = linking[sc, j * SB : (j + 1) * SB, :].astype(F32)
            columns[sc, :, j * SB : (j + 1) * SB] = block.T.astype(BF16)
    z_take(0, 0)
    z_take(0, 1)
    z_take(1, 0)
    z_take(1, 1)
    pass_right(0, 0)
    z_take(0, 2)
    z_take(1, 2)
    start_z()
    pass_left(0, 1)
    pass_left(0, 2)
    pass_right(0, 3)
    pass_right(1, 3)
    pass_left(1, 1)
    pass_right(1, 0)
    pass_left(1, 2)
    rest(0)
    solve_own(0)
    pass_z(1)
    rest(1)
    solve_own(1)

    def store(n, tile):
        partial[0, n] = tile[: SB // 2]
        partial[1, n] = tile[SB // 2 :]

    def wide(sc):
        return solved[sc, 0:3].reshape(3 * SB, ROWS)

    def store_wide(n, product, axis):
        for i in range(3):
            store(n + i, lax.slice_in_dim(product, i * SB, (i + 1) * SB, axis=axis))

    def pair(first):
        return solved_z[first : first + 2].reshape(2 * SB, ROWS)

    def gram(batch):
        near_below = z % 2 == 1
        below = upper == 1
        if batch == 0:
            store_wide(0, mm(solved[0, 0], wide(0)) + mm(solved[1, 0], wide(1)), 1)

            @pl.when(near_below)
            def _():
                store_wide(3, mm(solved_z[places[0]], wide(0)), 1)

            @pl.when(jnp.logical_not(near_below))
            def _():
                store_wide(3, mm(wide(1), solved_z[places[0]]), 0)
        elif batch == 1:
            @pl.when(below)
            def _():
                product = mm(pair(0), wide(0))
                store_wide(6, product[SB:], 1)
                store_wide(9, product[:SB], 1)

            @pl.when(jnp.logical_not(below))
            def _():
                product = mm(wide(1), pair(2))
                store_wide(6, product[:, :SB], 0)
                store_wide(9, product[:, SB:], 0)
        else:
            store(12, mm(solved[0, 0], solved[0, 3]) + mm(solved[1, 0], solved[1, 3]))

            @pl.when(near_below)
            def _():
                store(13, mm(solved_z[places[0]], solved[0, 3]))

            @pl.when(jnp.logical_not(near_below))
            def _():
                store(13, mm(solved[1, 3], solved_z[places[0]]))

            @pl.when(below)
            def _():
                product = mm(pair(0), solved[0, 3])
                store(14, product[SB:])
                store(15, product[:SB])

            @pl.when(jnp.logical_not(below))
            def _():
                product = mm(solved[1, 3], pair(2))
                store(14, product[:, :SB])
                store(15, product[:, SB:])

    def span(batch):
        return pl.ds(STARTS[batch], len(BATCHES[batch]))

    def to_core(batch):
        send(
            partial.at[1 - core, span(batch)],
            from_core.at[span(batch)],
            c_s.at[batch],
            c_r.at[batch],
            (s + 1 - 2 * core, g),
        )

    def of_y(yy, first=0, count=32):
        return pl.ds(pl.multiple_of((yy % NY) * 32 + first, 16), count)

    def both_cores(n, rows):
        return partial[core, n, rows, :] + from_core[n, rows, :]

    def over_tiles(batch, body):
        def step(n, carry):
            body(n)
            return carry

        lax.fori_loop(STARTS[batch], STARTS[batch] + len(BATCHES[batch]), step, 0)

    def along_y(batch):
        tiles = span(batch)
        await_bytes(from_core.at[tiles], c_r.at[batch])
        for k in (2, 1, 3):

            def body(n, k=k):
                to_y[k - 1, n] = both_cores(n, of_y(y + k)).astype(BF16)

            over_tiles(batch, body)
            send(
                to_y.at[k - 1, tiles],
                from_y.at[k - 1, tiles],
                y_s.at[batch, k - 1],
                y_r.at[batch, k - 1],
                (z_hi * 8 + ((y + k) % NY) * 2 + core, g),
            )

    def finish_y(batch):
        tiles = span(batch)
        for k in range(1, NY):
            await_bytes(from_y.at[k - 1, tiles], y_r.at[batch, k - 1])
        for n, (o, i) in enumerate(BATCHES[batch], STARTS[batch]):
            value = both_cores(n, of_y(y))
            for k in range(1, NY):
                value += from_y[k - 1, n].astype(F32)
            value = value.astype(BF16)
            if o == 3:
                slices[3, i] = value
            else:
                reduced[o, i] = value
                if i == 0:
                    near_x[0, o] = value

    def batch_z(ref, place, batch):
        return ref.at[place, pl.ds(WIDTH[batch][0], len(WIDTH[batch]))]

    def batch_x(ref, place, batch):
        return ref.at[place, pl.ds(OTHERS[batch][0], len(OTHERS[batch]))]

    def to_groups(batch):
        for o in OTHERS[batch]:
            send(
                batch_z(reduced, o, batch),
                batch_z(near_z, z, batch),
                nz_s.at[batch, o],
                nz_r.at[batch, z],
                (s, x * NZ + places[o]),
            )
        for i in WIDTH[batch]:
            if i:
                back = (0, 2, 1, 3)[i]
                send(
                    reduced.at[pl.ds(OTHERS[batch][0], len(OTHERS[batch])), i],
                    batch_x(near_x, back, batch),
                    nx_s.at[batch, i - 1],
                    nx_r.at[batch, back - 1],
                    (s, at_x(i) * NZ + z),
                )

    def from_groups(batch):
        for o in OTHERS[batch]:
            await_bytes(batch_z(near_z, places[o], batch), nz_r.at[batch, places[o]])
        for i in WIDTH[batch]:
            if i:
                await_bytes(batch_x(near_x, i, batch), nx_r.at[batch, i - 1])
        for o in OTHERS[batch]:
            for i in WIDTH[batch]:
                deliver(o, i)

    out_rows = pl.ds(pl.multiple_of(core * 128 + y * 32, 32), 32)

    def deliver(o, i):
        if o < 3:
            both = near_z[places[o], i].astype(F32) + near_x[i, o].astype(F32)
            slices[o, i] = both.astype(BF16)
        b = at_x(i) * NZ + places[o]
        piece = slices.at[o, i]
        target = final.at[z_hi, out_rows]

        @pl.when(b == s)
        def _():
            pltpu.make_async_copy(piece, target, fn_r.at[0]).start()

        @pl.when(b != s)
        def _():
            send(piece, target, fn_s.at[o * 4 + i], fn_r.at[0], (b, g))

    pass_z(2)
    solve_z(0)
    pass_x(0, 0)
    solve_z(1)
    pass_x(0, 1)
    pass_x(1, 0)
    pass_x(1, 1)
    gram(0)
    to_core(0)
    pass_z(3)
    solve_z(2)
    along_y(0)
    gram(1)
    to_core(1)
    far(0, 0)
    far(0, 1)
    along_y(1)
    far(1, 0)
    far(1, 1)
    gram(2)
    to_core(2)
    finish_y(0)
    to_groups(0)
    for i in range(3):
        deliver(3, i)
    along_y(2)
    finish_y(1)
    to_groups(1)
    from_groups(0)
    finish_y(2)
    to_groups(2)
    from_groups(1)
    deliver(3, 3)
    from_groups(2)

    for sc in range(2):

        @pl.when(z < NZ - 1)
        def _(sc=sc):
            await_bytes(factors.at[sc, g], fz_s.at[sc, 0])

        @pl.when(z > 0)
        def _(sc=sc):
            await_bytes(factors.at[sc, g], fz_s.at[sc, 1])

        for o in range(3):
            for onward in goes_on(places[o]):

                @pl.when(onward)
                def _(sc=sc, o=o):
                    await_bytes(factors.at[sc, g], fz_s.at[sc, 2 + o])

        for d in range(2):
            for k in range(4):
                await_bytes(factors.at[sc, g], fx_s.at[sc, d, k])
            for k in ((0, 3), (1, 2))[d]:
                await_bytes(factors.at[sc, g], ff_s.at[sc, d, k])
            for n in range(2):
                await_bytes(x_part(sc, 0, d), sx_s.at[sc, d, n])
                await_bytes(x_part(sc, 0, d, 0, SB // 2), sx_s.at[sc, d, 2 + n])
    for k in range(NZ - 1):

        @pl.when((z - k >= 0) & (z < NZ - 1))
        def _(k=k):
            for h in range(2):
                await_bytes(z_half(raw_z.at[0], h), zl_s.at[0, k, h])

        @pl.when((z + k <= NZ - 1) & (z > 0))
        def _(k=k):
            for h in range(2):
                await_bytes(z_half(raw_z.at[0], h), zl_s.at[1, k, h])

    for batch in range(3):
        await_bytes(from_core.at[span(batch)], c_s.at[batch])
    for batch in range(3):
        for k in range(NY - 1):
            await_bytes(from_y.at[k, span(batch)], y_s.at[batch, k])
    for batch in range(3):
        for o in OTHERS[batch]:
            await_bytes(batch_z(near_z, 0, batch), nz_s.at[batch, o])
        for i in WIDTH[batch]:
            if i:
                await_bytes(batch_x(near_x, 0, batch), nx_s.at[batch, i - 1])
    await_bytes(final, fn_r.at[0])

    @pl.when(z > s % NZ)
    def _():
        out[...] = ((final[0].astype(F32) + final[1].astype(F32)) * scaling).T

    @pl.when(z <= s % NZ)
    def _():
        out[...] = (final[0].astype(F32) + final[1].astype(F32)) * scaling

    for o in range(4):
        for i in range(4):

            @pl.when(at_x(i) * NZ + places[o] != s)
            def _(o=o, i=i):
                await_bytes(slices.at[0, 0], fn_s.at[o * 4 + i])


def local(linking, reach_count, diag_inverse, off_blocks, targets):
    scaling = 1.0 / math.sqrt(linking.shape[0] * 16 * ROWS)
    dma = pltpu.SemaphoreType.DMA
    vmem = pl.BlockSpec(memory_space=pltpu.VMEM)
    hbm = pl.BlockSpec(memory_space=pltpu.HBM)

    def body(*refs):
        kernel(scaling, *refs)

    operands = (jnp.swapaxes(targets, 1, 2), reach_count, linking, diag_inverse, off_blocks)
    return pl.pallas_call(
        body,
        out_shape=jax.ShapeDtypeStruct((SB, SB), F32),
        in_specs=[hbm] * 5,
        out_specs=vmem,
        scratch_shapes=[
            pltpu.SMEM((2, 2, NS), jnp.int32),
            pltpu.SMEM((2,), jnp.int32),
            pltpu.VMEM((2, ROWS, SB), BF16),
            pltpu.VMEM((2, 2, 16, SB), BF16),
            pltpu.VMEM((2, 16, PACK, 16, SB), BF16),
            pltpu.VMEM((2, NS - 1, SB, 3 * SB), BF16),
            pltpu.VMEM((2, SB, ROWS), BF16),
            pltpu.VMEM((2, NX, SB, ROWS), BF16),
            pltpu.VMEM((NZ, SB, ROWS), BF16),
            pltpu.VMEM((NZ, SB, ROWS), BF16),
            pltpu.VMEM((2, TILES, SB // 2, SB), F32),
            pltpu.VMEM((TILES, SB // 2, SB), F32),
            pltpu.VMEM((NY - 1, TILES, 32, SB), BF16),
            pltpu.VMEM((NY - 1, TILES, 32, SB), BF16),
            pltpu.VMEM((3, NX, 32, SB), BF16),
            pltpu.VMEM((NZ, NX, 32, SB), BF16),
            pltpu.VMEM((NX, 3, 32, SB), BF16),
            pltpu.VMEM((4, NX, 32, SB), BF16),
            pltpu.VMEM((2, SB, SB), BF16),
            dma((11,)),
            dma((2, 5)),
            dma((2, 4)),
            dma((2, 2, 4)),
            dma((2, 2, 4)),
            dma((2, 2, 4)),
            dma((2, 2, 4)),
            dma((2, 2, 4)),
            dma((2, 2, 4)),
            dma((2, 3, 2)),
            dma((2, 3, 2)),
            dma((3,)),
            dma((3,)),
            dma((3, 3)),
            dma((3, 3)),
            dma((3, 3)),
            dma((3, 4)),
            dma((3, 3)),
            dma((3, 3)),
            dma((16,)),
            dma((1,)),
        ],
        compiler_params=pltpu.CompilerParams(
            collective_id=0,
            has_side_effects=True,
            vmem_limit_bytes=44 * 1024 * 1024,
        ),
        cost_estimate=pl.CostEstimate(flops=3_000_000_000, bytes_accessed=5_000_000, transcendentals=0),
    )(*(pltpu.with_memory_space_constraint(a, pltpu.HBM) for a in operands))


def solution(mesh):
    return jax.shard_map(
        local,
        mesh=mesh,
        in_specs=(
            P("scen", None, "grp"),
            P("scen"),
            P("scen", None, "grp", None),
            P("scen", None, None, "grp", None),
            P("scen", None, None),
        ),
        out_specs=P("grp", "scen"),
        check_vma=False,
    )
```

```python
import math

import jax
import jax.numpy as jnp
from jax import lax
from jax.experimental import pallas as pl
from jax.experimental.pallas import tpu as pltpu
from jax.sharding import PartitionSpec as P

F32 = jnp.float32
BF16 = jnp.bfloat16
MESH = pl.DeviceIdType.MESH

NX = 4
NZ = 4
NY = 4
SB = 256
NS = 4
ROWS = NS * SB
HALF = ROWS // 2
PACK = 9
REL = (0, 1, 3, 2)

BATCHES = (
    ((3, 0), (3, 1), (3, 2), (0, 0), (0, 1), (0, 2)),
    ((1, 0), (1, 1), (1, 2), (2, 0), (2, 1), (2, 2)),
    ((3, 3), (0, 3), (1, 3), (2, 3)),
)
STARTS = (0, 6, 12)
OTHERS = ((0,), (1, 2), (0, 1, 2))
WIDTH = ((0, 1, 2), (0, 1, 2), (3,))
TILES = 16


def send(src, dst, send_sem, recv_sem, device):
    pltpu.make_async_remote_copy(
        src_ref=src,
        dst_ref=dst,
        send_sem=send_sem,
        recv_sem=recv_sem,
        device_id=device,
        device_id_type=MESH,
    ).start()


def await_bytes(ref, sem):
    pltpu.make_async_copy(ref, ref, sem).wait()


def flag(condition):
    return jnp.where(condition, 1.0, 0.0).astype(F32)


def mm(a, b):
    return lax.dot_general(a, b, (((1,), (1,)), ((), ())), preferred_element_type=F32)


def kernel(
    scaling,
    targets_hbm,
    reach_hbm,
    linking_hbm,
    diag,
    off,
    out,
    targets,
    reach,
    linking,
    choice,
    factors,
    lower,
    columns,
    solved,
    raw_z,
    solved_z,
    partial,
    from_core,
    to_y,
    from_y,
    reduced,
    near_z,
    near_x,
    slices,
    final,
    in_s,
    fz_s,
    fz_r,
    fx_s,
    fx_r,
    ff_s,
    ff_r,
    sx_s,
    sx_r,
    zl_s,
    zl_r,
    c_s,
    c_r,
    y_s,
    y_r,
    nz_s,
    nz_r,
    nx_s,
    nx_r,
    fn_s,
    fn_r,
):
    s = lax.axis_index("scen")
    g = lax.axis_index("grp")
    x, z = g // NZ, g % NZ
    core, y, z_hi = s % 2, (s // 2) % NY, s // (2 * NY)
    right_x, left_x, far_x = (x + 1) % NX, (x + 3) % NX, (x + 2) % NX
    right = (s, right_x * NZ + z)
    left = (s, left_x * NZ + z)
    upper = z // 2
    places = (z + 1 - 2 * (z % 2), 2 - upper, 3 - 3 * upper, z)

    def at_x(i):
        return (x + REL[i]) % NX

    barrier = pltpu.get_barrier_semaphore()

    def greet(k, carry):
        pl.semaphore_signal(barrier, inc=1, device_id=((s + k) % 16, g), device_id_type=MESH)
        return carry

    lax.fori_loop(1, 16, greet, 0)
    for k in range(1, NZ):
        pl.semaphore_signal(barrier, inc=1, device_id=(s, x * NZ + (z + k) % NZ), device_id_type=MESH)
    for k in range(1, NX):
        pl.semaphore_signal(barrier, inc=1, device_id=(s, ((x + k) % NX) * NZ + z), device_id_type=MESH)

    fetches = [(targets_hbm, targets), (reach_hbm, reach)]
    for sc in range(2):
        fetches.append((off.at[sc, 2], choice.at[sc]))
        fetches.append((diag.at[sc], factors.at[sc, g, pl.ds(0, NS)]))
        for i in range(2):
            fetches.append((off.at[sc, i], factors.at[sc, g, pl.ds(NS + 2 * i, 2)]))
    fetches.append((linking_hbm, linking))
    copies = [pltpu.make_async_copy(a, b, in_s.at[n]) for n, (a, b) in enumerate(fetches)]
    for copy in copies:
        copy.start()
    for copy in copies[:-1]:
        copy.wait()
    for sc in range(2):
        first = choice[sc, 0].astype(F32) * flag(targets[sc, 0, 2] == 3)
        second = choice[sc, 1].astype(F32) * flag(targets[sc, 1, 2] == 3)
        factors[sc, g, 8] = (first + second).astype(BF16)

    pl.semaphore_wait(barrier, 21)

    def shard(sc, xx, k):
        return factors.at[sc, xx * NZ + (z + k) % NZ]

    def x_send(sc, k):
        piece = shard(sc, x, k)
        send(piece, piece, fx_s.at[sc, 0, k], fx_r.at[sc, 0, k], right)
        send(piece, piece, fx_s.at[sc, 1, k], fx_r.at[sc, 1, k], left)

    def goes_on(q):
        return ((q < z) & (z < NZ - 1), (q > z) & (z > 0))

    def z_take(sc, o):
        q = places[o]
        piece = factors.at[sc, x * NZ + q]
        await_bytes(piece, fz_r.at[sc, q])
        for onward, device in zip(goes_on(q), ((s, g + 1), (s, g - 1))):

            @pl.when(onward)
            def _(device=device):
                send(piece, piece, fz_s.at[sc, 2 + o], fz_r.at[sc, q], device)

        x_send(sc, (q + NZ - z) % NZ)

    def pass_right(sc, k):
        piece = shard(sc, left_x, k)
        await_bytes(piece, fx_r.at[sc, 0, k])
        send(piece, piece, ff_s.at[sc, 0, k], ff_r.at[sc, 0, k], right)

    def pass_left(sc, k):
        piece = shard(sc, right_x, k)
        await_bytes(piece, fx_r.at[sc, 1, k])
        send(piece, piece, ff_s.at[sc, 1, k], ff_r.at[sc, 1, k], left)

    def rest(sc):
        for k in (1, 2):
            await_bytes(shard(sc, left_x, k), fx_r.at[sc, 0, k])
            await_bytes(shard(sc, far_x, k), ff_r.at[sc, 1, k])
        for k in (0, 3):
            await_bytes(shard(sc, right_x, k), fx_r.at[sc, 1, k])
            await_bytes(shard(sc, far_x, k), ff_r.at[sc, 0, k])

    def z_send(sc):
        own = factors.at[sc, g]

        @pl.when(z < NZ - 1)
        def _():
            send(own, own, fz_s.at[sc, 0], fz_r.at[sc, z], (s, g + 1))

        @pl.when(z > 0)
        def _():
            send(own, own, fz_s.at[sc, 1], fz_r.at[sc, z], (s, g - 1))

        x_send(sc, 0)

    def prepare(sc):
        for i in range(3):
            for j in range(i + 1, NS):
                if i == 2:
                    block = factors[sc, :, 8].reshape(SB, SB)
                else:
                    block = jnp.zeros((SB, SB), BF16)
                    for p in range(2):
                        chosen = flag(targets[sc, p, i] == j).astype(BF16)
                        block = block + factors[sc, :, 4 + 2 * i + p].reshape(SB, SB) * chosen
                lower[sc, j - 1, :, i * SB : (i + 1) * SB] = block

    def solve(sc, source, target, own=False, after=None):
        for j in range(NS):
            if own and j == 1:
                prepare(sc)
            here = slice(j * SB, (j + 1) * SB)
            residual = source[:, here].astype(F32) * flag(j >= NS - reach[sc])
            if j:
                residual = residual - mm(target[:, : j * SB], lower[sc, j - 1, :, : j * SB])
            inverse = factors[sc, :, j].reshape(SB, SB)
            target[:, here] = mm(residual.astype(BF16), inverse).astype(BF16)
            if after is not None:
                after(j)

    def x_part(sc, i, form, first=0, count=SB):
        return solved.at[sc, i, pl.ds(first, count), pl.ds(form * HALF, HALF)]

    def solve_own(sc):
        def after(j):
            if j % 2:
                form = j // 2
                own = x_part(sc, 0, form)
                send(own, x_part(sc, 2, form), sx_s.at[sc, form, 0], sx_r.at[sc, form, 0], right)
                send(own, x_part(sc, 1, form), sx_s.at[sc, form, 1], sx_r.at[sc, form, 1], left)

        solve(sc, columns.at[sc], solved.at[sc, 0], True, after)

    def pass_x(sc, form):
        await_bytes(x_part(sc, 2, form), sx_r.at[sc, form, 0])
        send(
            x_part(sc, 2, form, 0, SB // 2),
            x_part(sc, 3, form, 0, SB // 2),
            sx_s.at[sc, form, 2],
            sx_r.at[sc, form, 2],
            right,
        )
        await_bytes(x_part(sc, 1, form), sx_r.at[sc, form, 1])
        send(
            x_part(sc, 1, form, SB // 2, SB // 2),
            x_part(sc, 3, form, SB // 2, SB // 2),
            sx_s.at[sc, form, 3],
            sx_r.at[sc, form, 3],
            left,
        )

    def far(sc, form):
        for n in range(2):
            await_bytes(x_part(sc, 3, form, n * (SB // 2), SB // 2), sx_r.at[sc, form, 2 + n])

    def z_half(ref, h):
        return ref.at[pl.ds(h * (SB // 2), SB // 2)]

    def start_z():
        for h in range(2):

            @pl.when(z < NZ - 1)
            def _(h=h):
                send(z_half(columns.at[0], h), z_half(raw_z.at[z], h), zl_s.at[0, 0, h], zl_r.at[0, 0, h], (s, g + 1))

            @pl.when(z > 0)
            def _(h=h):
                send(z_half(columns.at[1], h), z_half(raw_z.at[z], h), zl_s.at[1, 0, h], zl_r.at[1, 0, h], (s, g - 1))

    def pass_z(k):
        for h in range(2):

            @pl.when(z - k >= 0)
            def _(h=h):
                block = z_half(raw_z.at[z - k], h)
                await_bytes(block, zl_r.at[0, k - 1, h])
                if k < NZ - 1:

                    @pl.when(z < NZ - 1)
                    def _():
                        send(block, block, zl_s.at[0, k, h], zl_r.at[0, k, h], (s, g + 1))

            @pl.when(z + k <= NZ - 1)
            def _(h=h):
                block = z_half(raw_z.at[z + k], h)
                await_bytes(block, zl_r.at[1, k - 1, h])
                if k < NZ - 1:

                    @pl.when(z > 0)
                    def _():
                        send(block, block, zl_s.at[1, k, h], zl_r.at[1, k, h], (s, g - 1))

    def solve_z(o):
        sc = (1 - z % 2) if o == 0 else (1 - upper)
        solve(sc, raw_z.at[places[o]], solved_z.at[places[o]])

    z_send(0)
    z_send(1)
    copies[-1].wait()
    for sc in range(2):
        for j in range(NS):
            block = linking[sc, j * SB : (j + 1) * SB, :].astype(F32)
            columns[sc, :, j * SB : (j + 1) * SB] = block.T.astype(BF16)
    z_take(0, 0)
    z_take(0, 1)
    z_take(1, 0)
    z_take(1, 1)
    pass_right(0, 0)
    z_take(0, 2)
    z_take(1, 2)
    start_z()
    pass_left(0, 1)
    pass_left(0, 2)
    pass_right(0, 3)
    pass_right(1, 3)
    pass_left(1, 1)
    pass_right(1, 0)
    pass_left(1, 2)
    rest(0)
    solve_own(0)
    pass_z(1)
    rest(1)
    solve_own(1)

    def store(n, tile):
        partial[0, n] = tile[: SB // 2]
        partial[1, n] = tile[SB // 2 :]

    def wide(sc):
        return solved[sc, 0:3].reshape(3 * SB, ROWS)

    def store_wide(n, product, axis):
        for i in range(3):
            store(n + i, lax.slice_in_dim(product, i * SB, (i + 1) * SB, axis=axis))

    def pair(first):
        return solved_z[first : first + 2].reshape(2 * SB, ROWS)

    def gram(batch):
        near_below = z % 2 == 1
        below = upper == 1
        if batch == 0:
            store_wide(0, mm(solved[0, 0], wide(0)) + mm(solved[1, 0], wide(1)), 1)

            @pl.when(near_below)
            def _():
                store_wide(3, mm(solved_z[places[0]], wide(0)), 1)

            @pl.when(jnp.logical_not(near_below))
            def _():
                store_wide(3, mm(wide(1), solved_z[places[0]]), 0)
        elif batch == 1:
            @pl.when(below)
            def _():
                product = mm(pair(0), wide(0))
                store_wide(6, product[SB:], 1)
                store_wide(9, product[:SB], 1)

            @pl.when(jnp.logical_not(below))
            def _():
                product = mm(wide(1), pair(2))
                store_wide(6, product[:, :SB], 0)
                store_wide(9, product[:, SB:], 0)
        else:
            store(12, mm(solved[0, 0], solved[0, 3]) + mm(solved[1, 0], solved[1, 3]))

            @pl.when(near_below)
            def _():
                store(13, mm(solved_z[places[0]], solved[0, 3]))

            @pl.when(jnp.logical_not(near_below))
            def _():
                store(13, mm(solved[1, 3], solved_z[places[0]]))

            @pl.when(below)
            def _():
                product = mm(pair(0), solved[0, 3])
                store(14, product[SB:])
                store(15, product[:SB])

            @pl.when(jnp.logical_not(below))
            def _():
                product = mm(solved[1, 3], pair(2))
                store(14, product[:, :SB])
                store(15, product[:, SB:])

    def span(batch):
        return pl.ds(STARTS[batch], len(BATCHES[batch]))

    def to_core(batch):
        send(
            partial.at[1 - core, span(batch)],
            from_core.at[span(batch)],
            c_s.at[batch],
            c_r.at[batch],
            (s + 1 - 2 * core, g),
        )

    def of_y(yy, first=0, count=32):
        return pl.ds(pl.multiple_of((yy % NY) * 32 + first, 16), count)

    def both_cores(n, rows):
        return partial[core, n, rows, :] + from_core[n, rows, :]

    def over_tiles(batch, body):
        def step(n, carry):
            body(n)
            return carry

        lax.fori_loop(STARTS[batch], STARTS[batch] + len(BATCHES[batch]), step, 0)

    def along_y(batch):
        tiles = span(batch)
        await_bytes(from_core.at[tiles], c_r.at[batch])
        for k in (2, 1, 3):

            def body(n, k=k):
                to_y[k - 1, n] = both_cores(n, of_y(y + k)).astype(BF16)

            over_tiles(batch, body)
            send(
                to_y.at[k - 1, tiles],
                from_y.at[k - 1, tiles],
                y_s.at[batch, k - 1],
                y_r.at[batch, k - 1],
                (z_hi * 8 + ((y + k) % NY) * 2 + core, g),
            )

    def finish_y(batch):
        tiles = span(batch)
        for k in range(1, NY):
            await_bytes(from_y.at[k - 1, tiles], y_r.at[batch, k - 1])
        for n, (o, i) in enumerate(BATCHES[batch], STARTS[batch]):
            value = both_cores(n, of_y(y))
            for k in range(1, NY):
                value += from_y[k - 1, n].astype(F32)
            value = value.astype(BF16)
            if o == 3:
                slices[3, i] = value
            else:
                reduced[o, i] = value
                if i == 0:
                    near_x[0, o] = value

    def batch_z(ref, place, batch):
        return ref.at[place, pl.ds(WIDTH[batch][0], len(WIDTH[batch]))]

    def batch_x(ref, place, batch):
        return ref.at[place, pl.ds(OTHERS[batch][0], len(OTHERS[batch]))]

    def to_groups(batch):
        for o in OTHERS[batch]:
            send(
                batch_z(reduced, o, batch),
                batch_z(near_z, z, batch),
                nz_s.at[batch, o],
                nz_r.at[batch, z],
                (s, x * NZ + places[o]),
            )
        for i in WIDTH[batch]:
            if i:
                back = (0, 2, 1, 3)[i]
                send(
                    reduced.at[pl.ds(OTHERS[batch][0], len(OTHERS[batch])), i],
                    batch_x(near_x, back, batch),
                    nx_s.at[batch, i - 1],
                    nx_r.at[batch, back - 1],
                    (s, at_x(i) * NZ + z),
                )

    def from_groups(batch):
        for n, i in enumerate(WIDTH[batch]):
            if i:
                await_bytes(batch_x(near_x, i, batch), nx_r.at[batch, i - 1])
            for o in OTHERS[batch]:
                if n == 0:
                    await_bytes(batch_z(near_z, places[o], batch), nz_r.at[batch, places[o]])
                deliver(o, i)

    out_rows = pl.ds(pl.multiple_of(core * 128 + y * 32, 32), 32)

    def deliver(o, i):
        if o < 3:
            both = near_z[places[o], i].astype(F32) + near_x[i, o].astype(F32)
            slices[o, i] = both.astype(BF16)
        b = at_x(i) * NZ + places[o]
        piece = slices.at[o, i]
        target = final.at[z_hi, out_rows]

        @pl.when(b == s)
        def _():
            pltpu.make_async_copy(piece, target, fn_r.at[0]).start()

        @pl.when(b != s)
        def _():
            send(piece, target, fn_s.at[o * 4 + i], fn_r.at[0], (b, g))

    pass_z(2)
    solve_z(0)
    pass_x(0, 0)
    solve_z(1)
    pass_x(0, 1)
    pass_x(1, 0)
    pass_x(1, 1)
    gram(0)
    to_core(0)
    pass_z(3)
    solve_z(2)
    along_y(0)
    gram(1)
    to_core(1)
    far(0, 0)
    far(0, 1)
    along_y(1)
    far(1, 0)
    far(1, 1)
    gram(2)
    to_core(2)
    finish_y(0)
    to_groups(0)
    for i in range(3):
        deliver(3, i)
    along_y(2)
    from_groups(0)
    finish_y(1)
    to_groups(1)
    finish_y(2)
    to_groups(2)
    from_groups(1)
    deliver(3, 3)
    from_groups(2)

    for sc in range(2):

        @pl.when(z < NZ - 1)
        def _(sc=sc):
            await_bytes(factors.at[sc, g], fz_s.at[sc, 0])

        @pl.when(z > 0)
        def _(sc=sc):
            await_bytes(factors.at[sc, g], fz_s.at[sc, 1])

        for o in range(3):
            for onward in goes_on(places[o]):

                @pl.when(onward)
                def _(sc=sc, o=o):
                    await_bytes(factors.at[sc, g], fz_s.at[sc, 2 + o])

        for d in range(2):
            for k in range(4):
                await_bytes(factors.at[sc, g], fx_s.at[sc, d, k])
            for k in ((0, 3), (1, 2))[d]:
                await_bytes(factors.at[sc, g], ff_s.at[sc, d, k])
            for n in range(2):
                await_bytes(x_part(sc, 0, d), sx_s.at[sc, d, n])
                await_bytes(x_part(sc, 0, d, 0, SB // 2), sx_s.at[sc, d, 2 + n])
    for k in range(NZ - 1):

        @pl.when((z - k >= 0) & (z < NZ - 1))
        def _(k=k):
            for h in range(2):
                await_bytes(z_half(raw_z.at[0], h), zl_s.at[0, k, h])

        @pl.when((z + k <= NZ - 1) & (z > 0))
        def _(k=k):
            for h in range(2):
                await_bytes(z_half(raw_z.at[0], h), zl_s.at[1, k, h])

    for batch in range(3):
        await_bytes(from_core.at[span(batch)], c_s.at[batch])
    for batch in range(3):
        for k in range(NY - 1):
            await_bytes(from_y.at[k, span(batch)], y_s.at[batch, k])
    for batch in range(3):
        for o in OTHERS[batch]:
            await_bytes(batch_z(near_z, 0, batch), nz_s.at[batch, o])
        for i in WIDTH[batch]:
            if i:
                await_bytes(batch_x(near_x, 0, batch), nx_s.at[batch, i - 1])
    await_bytes(final, fn_r.at[0])

    @pl.when(z > s % NZ)
    def _():
        out[...] = ((final[0].astype(F32) + final[1].astype(F32)) * scaling).T

    @pl.when(z <= s % NZ)
    def _():
        out[...] = (final[0].astype(F32) + final[1].astype(F32)) * scaling

    for o in range(4):
        for i in range(4):

            @pl.when(at_x(i) * NZ + places[o] != s)
            def _(o=o, i=i):
                await_bytes(slices.at[0, 0], fn_s.at[o * 4 + i])


def local(linking, reach_count, diag_inverse, off_blocks, targets):
    scaling = 1.0 / math.sqrt(linking.shape[0] * 16 * ROWS)
    dma = pltpu.SemaphoreType.DMA
    vmem = pl.BlockSpec(memory_space=pltpu.VMEM)
    hbm = pl.BlockSpec(memory_space=pltpu.HBM)

    def body(*refs):
        kernel(scaling, *refs)

    operands = (jnp.swapaxes(targets, 1, 2), reach_count, linking, diag_inverse, off_blocks)
    return pl.pallas_call(
        body,
        out_shape=jax.ShapeDtypeStruct((SB, SB), F32),
        in_specs=[hbm] * 5,
        out_specs=vmem,
        scratch_shapes=[
            pltpu.SMEM((2, 2, NS), jnp.int32),
            pltpu.SMEM((2,), jnp.int32),
            pltpu.VMEM((2, ROWS, SB), BF16),
            pltpu.VMEM((2, 2, 16, SB), BF16),
            pltpu.VMEM((2, 16, PACK, 16, SB), BF16),
            pltpu.VMEM((2, NS - 1, SB, 3 * SB), BF16),
            pltpu.VMEM((2, SB, ROWS), BF16),
            pltpu.VMEM((2, NX, SB, ROWS), BF16),
            pltpu.VMEM((NZ, SB, ROWS), BF16),
            pltpu.VMEM((NZ, SB, ROWS), BF16),
            pltpu.VMEM((2, TILES, SB // 2, SB), F32),
            pltpu.VMEM((TILES, SB // 2, SB), F32),
            pltpu.VMEM((NY - 1, TILES, 32, SB), BF16),
            pltpu.VMEM((NY - 1, TILES, 32, SB), BF16),
            pltpu.VMEM((3, NX, 32, SB), BF16),
            pltpu.VMEM((NZ, NX, 32, SB), BF16),
            pltpu.VMEM((NX, 3, 32, SB), BF16),
            pltpu.VMEM((4, NX, 32, SB), BF16),
            pltpu.VMEM((2, SB, SB), BF16),
            dma((11,)),
            dma((2, 5)),
            dma((2, 4)),
            dma((2, 2, 4)),
            dma((2, 2, 4)),
            dma((2, 2, 4)),
            dma((2, 2, 4)),
            dma((2, 2, 4)),
            dma((2, 2, 4)),
            dma((2, 3, 2)),
            dma((2, 3, 2)),
            dma((3,)),
            dma((3,)),
            dma((3, 3)),
            dma((3, 3)),
            dma((3, 3)),
            dma((3, 4)),
            dma((3, 3)),
            dma((3, 3)),
            dma((16,)),
            dma((1,)),
        ],
        compiler_params=pltpu.CompilerParams(
            collective_id=0,
            has_side_effects=True,
            vmem_limit_bytes=44 * 1024 * 1024,
        ),
        cost_estimate=pl.CostEstimate(flops=3_000_000_000, bytes_accessed=5_000_000, transcendentals=0),
    )(*(pltpu.with_memory_space_constraint(a, pltpu.HBM) for a in operands))


def solution(mesh):
    return jax.shard_map(
        local,
        mesh=mesh,
        in_specs=(
            P("scen", None, "grp"),
            P("scen"),
            P("scen", None, "grp", None),
            P("scen", None, None, "grp", None),
            P("scen", None, None),
        ),
        out_specs=P("grp", "scen"),
        check_vma=False,
    )
```

```python
import math

import jax
import jax.numpy as jnp
from jax import lax
from jax.experimental import pallas as pl
from jax.experimental.pallas import tpu as pltpu
from jax.sharding import PartitionSpec as P

F32 = jnp.float32
BF16 = jnp.bfloat16
MESH = pl.DeviceIdType.MESH

NX = 4
NZ = 4
NY = 4
SB = 256
NS = 4
ROWS = NS * SB
HALF = ROWS // 2
PACK = 9
REL = (0, 1, 3, 2)

BATCHES = (
    ((3, 0), (3, 1), (3, 2), (0, 0), (0, 1), (0, 2)),
    ((1, 0), (1, 1), (1, 2), (2, 0), (2, 1), (2, 2)),
    ((3, 3), (0, 3), (1, 3), (2, 3)),
)
STARTS = (0, 6, 12)
OTHERS = ((0,), (1, 2), (0, 1, 2))
WIDTH = ((0, 1, 2), (0, 1, 2), (3,))
TILES = 16


def send(src, dst, send_sem, recv_sem, device):
    pltpu.make_async_remote_copy(
        src_ref=src,
        dst_ref=dst,
        send_sem=send_sem,
        recv_sem=recv_sem,
        device_id=device,
        device_id_type=MESH,
    ).start()


def await_bytes(ref, sem):
    pltpu.make_async_copy(ref, ref, sem).wait()


def flag(condition):
    return jnp.where(condition, 1.0, 0.0).astype(F32)


def mm(a, b):
    return lax.dot_general(a, b, (((1,), (1,)), ((), ())), preferred_element_type=F32)


def kernel(
    scaling,
    targets_hbm,
    reach_hbm,
    linking_hbm,
    diag,
    off,
    out,
    targets,
    reach,
    linking,
    choice,
    factors,
    lower,
    columns,
    solved,
    raw_z,
    solved_z,
    partial,
    from_core,
    to_y,
    from_y,
    reduced,
    near_z,
    near_x,
    slices,
    final,
    in_s,
    fz_s,
    fz_r,
    fx_s,
    fx_r,
    ff_s,
    ff_r,
    sx_s,
    sx_r,
    zl_s,
    zl_r,
    c_s,
    c_r,
    y_s,
    y_r,
    nz_s,
    nz_r,
    nx_s,
    nx_r,
    fn_s,
    fn_r,
):
    s = lax.axis_index("scen")
    g = lax.axis_index("grp")
    x, z = g // NZ, g % NZ
    core, y, z_hi = s % 2, (s // 2) % NY, s // (2 * NY)
    right_x, left_x, far_x = (x + 1) % NX, (x + 3) % NX, (x + 2) % NX
    right = (s, right_x * NZ + z)
    left = (s, left_x * NZ + z)
    upper = z // 2
    places = (z + 1 - 2 * (z % 2), 2 - upper, 3 - 3 * upper, z)

    def at_x(i):
        return (x + REL[i]) % NX

    barrier = pltpu.get_barrier_semaphore()

    def greet(k, carry):
        pl.semaphore_signal(barrier, inc=1, device_id=((s + k) % 16, g), device_id_type=MESH)
        return carry

    lax.fori_loop(1, 16, greet, 0)
    for k in range(1, NZ):
        pl.semaphore_signal(barrier, inc=1, device_id=(s, x * NZ + (z + k) % NZ), device_id_type=MESH)
    for k in range(1, NX):
        pl.semaphore_signal(barrier, inc=1, device_id=(s, ((x + k) % NX) * NZ + z), device_id_type=MESH)

    fetches = [(targets_hbm, targets), (reach_hbm, reach)]
    for sc in range(2):
        fetches.append((off.at[sc, 2], choice.at[sc]))
        fetches.append((diag.at[sc], factors.at[sc, g, pl.ds(0, NS)]))
        for i in range(2):
            fetches.append((off.at[sc, i], factors.at[sc, g, pl.ds(NS + 2 * i, 2)]))
    fetches.append((linking_hbm, linking))
    copies = [pltpu.make_async_copy(a, b, in_s.at[n]) for n, (a, b) in enumerate(fetches)]
    for copy in copies:
        copy.start()
    for copy in copies[:-1]:
        copy.wait()
    for sc in range(2):
        first = choice[sc, 0].astype(F32) * flag(targets[sc, 0, 2] == 3)
        second = choice[sc, 1].astype(F32) * flag(targets[sc, 1, 2] == 3)
        factors[sc, g, 8] = (first + second).astype(BF16)

    pl.semaphore_wait(barrier, 21)

    def shard(sc, xx, k):
        return factors.at[sc, xx * NZ + (z + k) % NZ]

    def x_send(sc, k):
        piece = shard(sc, x, k)
        send(piece, piece, fx_s.at[sc, 0, k], fx_r.at[sc, 0, k], right)
        send(piece, piece, fx_s.at[sc, 1, k], fx_r.at[sc, 1, k], left)

    def goes_on(q):
        return ((q < z) & (z < NZ - 1), (q > z) & (z > 0))

    def z_take(sc, o):
        q = places[o]
        piece = factors.at[sc, x * NZ + q]
        await_bytes(piece, fz_r.at[sc, q])
        for onward, device in zip(goes_on(q), ((s, g + 1), (s, g - 1))):

            @pl.when(onward)
            def _(device=device):
                send(piece, piece, fz_s.at[sc, 2 + o], fz_r.at[sc, q], device)

        x_send(sc, (q + NZ - z) % NZ)

    def pass_right(sc, k):
        piece = shard(sc, left_x, k)
        await_bytes(piece, fx_r.at[sc, 0, k])
        send(piece, piece, ff_s.at[sc, 0, k], ff_r.at[sc, 0, k], right)

    def pass_left(sc, k):
        piece = shard(sc, right_x, k)
        await_bytes(piece, fx_r.at[sc, 1, k])
        send(piece, piece, ff_s.at[sc, 1, k], ff_r.at[sc, 1, k], left)

    def rest(sc):
        for k in (1, 2):
            await_bytes(shard(sc, left_x, k), fx_r.at[sc, 0, k])
            await_bytes(shard(sc, far_x, k), ff_r.at[sc, 1, k])
        for k in (0, 3):
            await_bytes(shard(sc, right_x, k), fx_r.at[sc, 1, k])
            await_bytes(shard(sc, far_x, k), ff_r.at[sc, 0, k])

    def z_send(sc):
        own = factors.at[sc, g]

        @pl.when(z < NZ - 1)
        def _():
            send(own, own, fz_s.at[sc, 0], fz_r.at[sc, z], (s, g + 1))

        @pl.when(z > 0)
        def _():
            send(own, own, fz_s.at[sc, 1], fz_r.at[sc, z], (s, g - 1))

        x_send(sc, 0)

    def prepare(sc):
        for i in range(3):
            for j in range(i + 1, NS):
                if i == 2:
                    block = factors[sc, :, 8].reshape(SB, SB)
                else:
                    block = jnp.zeros((SB, SB), BF16)
                    for p in range(2):
                        chosen = flag(targets[sc, p, i] == j).astype(BF16)
                        block = block + factors[sc, :, 4 + 2 * i + p].reshape(SB, SB) * chosen
                lower[sc, j - 1, :, i * SB : (i + 1) * SB] = block

    def solve(sc, source, target, own=False, after=None):
        for j in range(NS):
            if own and j == 1:
                prepare(sc)
            here = slice(j * SB, (j + 1) * SB)
            residual = source[:, here].astype(F32) * flag(j >= NS - reach[sc])
            if j:
                residual = residual - mm(target[:, : j * SB], lower[sc, j - 1, :, : j * SB])
            inverse = factors[sc, :, j].reshape(SB, SB)
            target[:, here] = mm(residual.astype(BF16), inverse).astype(BF16)
            if after is not None:
                after(j)

    def x_part(sc, i, form, first=0, count=SB):
        return solved.at[sc, i, pl.ds(first, count), pl.ds(form * HALF, HALF)]

    def solve_own(sc):
        def after(j):
            if j % 2:
                form = j // 2
                own = x_part(sc, 0, form)
                send(own, x_part(sc, 2, form), sx_s.at[sc, form, 0], sx_r.at[sc, form, 0], right)
                send(own, x_part(sc, 1, form), sx_s.at[sc, form, 1], sx_r.at[sc, form, 1], left)

        solve(sc, columns.at[sc], solved.at[sc, 0], True, after)

    def pass_x(sc, form):
        await_bytes(x_part(sc, 2, form), sx_r.at[sc, form, 0])
        send(
            x_part(sc, 2, form, 0, SB // 2),
            x_part(sc, 3, form, 0, SB // 2),
            sx_s.at[sc, form, 2],
            sx_r.at[sc, form, 2],
            right,
        )
        await_bytes(x_part(sc, 1, form), sx_r.at[sc, form, 1])
        send(
            x_part(sc, 1, form, SB // 2, SB // 2),
            x_part(sc, 3, form, SB // 2, SB // 2),
            sx_s.at[sc, form, 3],
            sx_r.at[sc, form, 3],
            left,
        )

    def far(sc, form):
        for n in range(2):
            await_bytes(x_part(sc, 3, form, n * (SB // 2), SB // 2), sx_r.at[sc, form, 2 + n])

    def z_half(ref, h):
        return ref.at[pl.ds(h * (SB // 2), SB // 2)]

    def start_z():
        for h in range(2):

            @pl.when(z < NZ - 1)
            def _(h=h):
                send(z_half(columns.at[0], h), z_half(raw_z.at[z], h), zl_s.at[0, 0, h], zl_r.at[0, 0, h], (s, g + 1))

            @pl.when(z > 0)
            def _(h=h):
                send(z_half(columns.at[1], h), z_half(raw_z.at[z], h), zl_s.at[1, 0, h], zl_r.at[1, 0, h], (s, g - 1))

    def pass_z(k):
        for h in range(2):

            @pl.when(z - k >= 0)
            def _(h=h):
                block = z_half(raw_z.at[z - k], h)
                await_bytes(block, zl_r.at[0, k - 1, h])
                if k < NZ - 1:

                    @pl.when(z < NZ - 1)
                    def _():
                        send(block, block, zl_s.at[0, k, h], zl_r.at[0, k, h], (s, g + 1))

            @pl.when(z + k <= NZ - 1)
            def _(h=h):
                block = z_half(raw_z.at[z + k], h)
                await_bytes(block, zl_r.at[1, k - 1, h])
                if k < NZ - 1:

                    @pl.when(z > 0)
                    def _():
                        send(block, block, zl_s.at[1, k, h], zl_r.at[1, k, h], (s, g - 1))

    def solve_z(o):
        sc = (1 - z % 2) if o == 0 else (1 - upper)
        solve(sc, raw_z.at[places[o]], solved_z.at[places[o]])

    z_send(0)
    z_send(1)
    copies[-1].wait()
    for sc in range(2):
        for j in range(NS):
            block = linking[sc, j * SB : (j + 1) * SB, :].astype(F32)
            columns[sc, :, j * SB : (j + 1) * SB] = block.T.astype(BF16)
    z_take(0, 0)
    z_take(0, 1)
    z_take(1, 0)
    z_take(1, 1)
    pass_right(0, 0)
    z_take(0, 2)
    z_take(1, 2)
    start_z()
    pass_left(0, 1)
    pass_left(0, 2)
    pass_right(0, 3)
    pass_right(1, 3)
    pass_left(1, 1)
    pass_right(1, 0)
    pass_left(1, 2)
    rest(0)
    solve_own(0)
    pass_z(1)
    rest(1)
    solve_own(1)

    def store(n, tile):
        partial[0, n] = tile[: SB // 2]
        partial[1, n] = tile[SB // 2 :]

    def wide(sc):
        return solved[sc, 0:3].reshape(3 * SB, ROWS)

    def store_wide(n, product, axis):
        for i in range(3):
            store(n + i, lax.slice_in_dim(product, i * SB, (i + 1) * SB, axis=axis))

    def pair(first):
        return solved_z[first : first + 2].reshape(2 * SB, ROWS)

    def gram(batch):
        near_below = z % 2 == 1
        below = upper == 1
        if batch == 0:
            store_wide(0, mm(solved[0, 0], wide(0)) + mm(solved[1, 0], wide(1)), 1)

            @pl.when(near_below)
            def _():
                store_wide(3, mm(solved_z[places[0]], wide(0)), 1)

            @pl.when(jnp.logical_not(near_below))
            def _():
                store_wide(3, mm(wide(1), solved_z[places[0]]), 0)
        elif batch == 1:
            @pl.when(below)
            def _():
                product = mm(pair(0), wide(0))
                store_wide(6, product[SB:], 1)
                store_wide(9, product[:SB], 1)

            @pl.when(jnp.logical_not(below))
            def _():
                product = mm(wide(1), pair(2))
                store_wide(6, product[:, :SB], 0)
                store_wide(9, product[:, SB:], 0)
        else:
            store(12, mm(solved[0, 0], solved[0, 3]) + mm(solved[1, 0], solved[1, 3]))

            @pl.when(near_below)
            def _():
                store(13, mm(solved_z[places[0]], solved[0, 3]))

            @pl.when(jnp.logical_not(near_below))
            def _():
                store(13, mm(solved[1, 3], solved_z[places[0]]))

            @pl.when(below)
            def _():
                product = mm(pair(0), solved[0, 3])
                store(14, product[SB:])
                store(15, product[:SB])

            @pl.when(jnp.logical_not(below))
            def _():
                product = mm(solved[1, 3], pair(2))
                store(14, product[:, :SB])
                store(15, product[:, SB:])

    def span(batch):
        return pl.ds(STARTS[batch], len(BATCHES[batch]))

    def to_core(batch):
        send(
            partial.at[1 - core, span(batch)],
            from_core.at[span(batch)],
            c_s.at[batch],
            c_r.at[batch],
            (s + 1 - 2 * core, g),
        )

    def of_y(yy, first=0, count=32):
        return pl.ds(pl.multiple_of((yy % NY) * 32 + first, 16), count)

    def both_cores(n, rows):
        return partial[core, n, rows, :] + from_core[n, rows, :]

    def over_tiles(batch, body):
        def step(n, carry):
            body(n)
            return carry

        lax.fori_loop(STARTS[batch], STARTS[batch] + len(BATCHES[batch]), step, 0)

    def along_y(batch):
        tiles = span(batch)
        await_bytes(from_core.at[tiles], c_r.at[batch])
        for k in (2, 1, 3):

            def body(n, k=k):
                to_y[k - 1, n] = both_cores(n, of_y(y + k)).astype(BF16)

            over_tiles(batch, body)
            send(
                to_y.at[k - 1, tiles],
                from_y.at[k - 1, tiles],
                y_s.at[batch, k - 1],
                y_r.at[batch, k - 1],
                (z_hi * 8 + ((y + k) % NY) * 2 + core, g),
            )

    def finish_y(batch):
        tiles = span(batch)
        for k in range(1, NY):
            await_bytes(from_y.at[k - 1, tiles], y_r.at[batch, k - 1])
        for n, (o, i) in enumerate(BATCHES[batch], STARTS[batch]):
            value = both_cores(n, of_y(y))
            for k in range(1, NY):
                value += from_y[k - 1, n].astype(F32)
            value = value.astype(BF16)
            if o == 3:
                slices[3, i] = value
            else:
                reduced[o, i] = value
                if i == 0:
                    near_x[0, o] = value

    def batch_z(ref, place, batch):
        return ref.at[place, pl.ds(WIDTH[batch][0], len(WIDTH[batch]))]

    def batch_x(ref, place, batch):
        return ref.at[place, pl.ds(OTHERS[batch][0], len(OTHERS[batch]))]

    def to_groups(batch):
        for o in OTHERS[batch]:
            send(
                batch_z(reduced, o, batch),
                batch_z(near_z, z, batch),
                nz_s.at[batch, o],
                nz_r.at[batch, z],
                (s, x * NZ + places[o]),
            )
        for i in WIDTH[batch]:
            if i:
                back = (0, 2, 1, 3)[i]
                send(
                    reduced.at[pl.ds(OTHERS[batch][0], len(OTHERS[batch])), i],
                    batch_x(near_x, back, batch),
                    nx_s.at[batch, i - 1],
                    nx_r.at[batch, back - 1],
                    (s, at_x(i) * NZ + z),
                )

    def from_groups(batch):
        for n, i in enumerate(WIDTH[batch]):
            if i:
                await_bytes(batch_x(near_x, i, batch), nx_r.at[batch, i - 1])
            for o in OTHERS[batch]:
                if n == 0:
                    await_bytes(batch_z(near_z, places[o], batch), nz_r.at[batch, places[o]])
                deliver(o, i)

    out_rows = pl.ds(pl.multiple_of(core * 128 + y * 32, 32), 32)

    def deliver(o, i):
        if o < 3:
            both = near_z[places[o], i].astype(F32) + near_x[i, o].astype(F32)
            slices[o, i] = both.astype(BF16)
        b = at_x(i) * NZ + places[o]
        piece = slices.at[o, i]
        target = final.at[z_hi, out_rows]

        @pl.when(b == s)
        def _():
            pltpu.make_async_copy(piece, target, fn_r.at[0]).start()

        @pl.when(b != s)
        def _():
            send(piece, target, fn_s.at[o * 4 + i], fn_r.at[0], (b, g))

    pass_z(2)
    solve_z(0)
    pass_x(0, 0)
    solve_z(1)
    pass_x(0, 1)
    pass_x(1, 0)
    pass_x(1, 1)
    gram(0)
    to_core(0)
    pass_z(3)
    solve_z(2)
    along_y(0)
    gram(1)
    to_core(1)
    far(0, 0)
    far(0, 1)
    along_y(1)
    finish_y(0)
    to_groups(0)
    for i in range(3):
        deliver(3, i)
    far(1, 0)
    far(1, 1)
    gram(2)
    to_core(2)
    along_y(2)
    from_groups(0)
    finish_y(1)
    to_groups(1)
    finish_y(2)
    to_groups(2)
    from_groups(1)
    deliver(3, 3)
    from_groups(2)

    for sc in range(2):

        @pl.when(z < NZ - 1)
        def _(sc=sc):
            await_bytes(factors.at[sc, g], fz_s.at[sc, 0])

        @pl.when(z > 0)
        def _(sc=sc):
            await_bytes(factors.at[sc, g], fz_s.at[sc, 1])

        for o in range(3):
            for onward in goes_on(places[o]):

                @pl.when(onward)
                def _(sc=sc, o=o):
                    await_bytes(factors.at[sc, g], fz_s.at[sc, 2 + o])

        for d in range(2):
            for k in range(4):
                await_bytes(factors.at[sc, g], fx_s.at[sc, d, k])
            for k in ((0, 3), (1, 2))[d]:
                await_bytes(factors.at[sc, g], ff_s.at[sc, d, k])
            for n in range(2):
                await_bytes(x_part(sc, 0, d), sx_s.at[sc, d, n])
                await_bytes(x_part(sc, 0, d, 0, SB // 2), sx_s.at[sc, d, 2 + n])
    for k in range(NZ - 1):

        @pl.when((z - k >= 0) & (z < NZ - 1))
        def _(k=k):
            for h in range(2):
                await_bytes(z_half(raw_z.at[0], h), zl_s.at[0, k, h])

        @pl.when((z + k <= NZ - 1) & (z > 0))
        def _(k=k):
            for h in range(2):
                await_bytes(z_half(raw_z.at[0], h), zl_s.at[1, k, h])

    for batch in range(3):
        await_bytes(from_core.at[span(batch)], c_s.at[batch])
    for batch in range(3):
        for k in range(NY - 1):
            await_bytes(from_y.at[k, span(batch)], y_s.at[batch, k])
    for batch in range(3):
        for o in OTHERS[batch]:
            await_bytes(batch_z(near_z, 0, batch), nz_s.at[batch, o])
        for i in WIDTH[batch]:
            if i:
                await_bytes(batch_x(near_x, 0, batch), nx_s.at[batch, i - 1])
    await_bytes(final, fn_r.at[0])

    @pl.when(z > s % NZ)
    def _():
        out[...] = ((final[0].astype(F32) + final[1].astype(F32)) * scaling).T

    @pl.when(z <= s % NZ)
    def _():
        out[...] = (final[0].astype(F32) + final[1].astype(F32)) * scaling

    for o in range(4):
        for i in range(4):

            @pl.when(at_x(i) * NZ + places[o] != s)
            def _(o=o, i=i):
                await_bytes(slices.at[0, 0], fn_s.at[o * 4 + i])


def local(linking, reach_count, diag_inverse, off_blocks, targets):
    scaling = 1.0 / math.sqrt(linking.shape[0] * 16 * ROWS)
    dma = pltpu.SemaphoreType.DMA
    vmem = pl.BlockSpec(memory_space=pltpu.VMEM)
    hbm = pl.BlockSpec(memory_space=pltpu.HBM)

    def body(*refs):
        kernel(scaling, *refs)

    operands = (jnp.swapaxes(targets, 1, 2), reach_count, linking, diag_inverse, off_blocks)
    return pl.pallas_call(
        body,
        out_shape=jax.ShapeDtypeStruct((SB, SB), F32),
        in_specs=[hbm] * 5,
        out_specs=vmem,
        scratch_shapes=[
            pltpu.SMEM((2, 2, NS), jnp.int32),
            pltpu.SMEM((2,), jnp.int32),
            pltpu.VMEM((2, ROWS, SB), BF16),
            pltpu.VMEM((2, 2, 16, SB), BF16),
            pltpu.VMEM((2, 16, PACK, 16, SB), BF16),
            pltpu.VMEM((2, NS - 1, SB, 3 * SB), BF16),
            pltpu.VMEM((2, SB, ROWS), BF16),
            pltpu.VMEM((2, NX, SB, ROWS), BF16),
            pltpu.VMEM((NZ, SB, ROWS), BF16),
            pltpu.VMEM((NZ, SB, ROWS), BF16),
            pltpu.VMEM((2, TILES, SB // 2, SB), F32),
            pltpu.VMEM((TILES, SB // 2, SB), F32),
            pltpu.VMEM((NY - 1, TILES, 32, SB), BF16),
            pltpu.VMEM((NY - 1, TILES, 32, SB), BF16),
            pltpu.VMEM((3, NX, 32, SB), BF16),
            pltpu.VMEM((NZ, NX, 32, SB), BF16),
            pltpu.VMEM((NX, 3, 32, SB), BF16),
            pltpu.VMEM((4, NX, 32, SB), BF16),
            pltpu.VMEM((2, SB, SB), BF16),
            dma((11,)),
            dma((2, 5)),
            dma((2, 4)),
            dma((2, 2, 4)),
            dma((2, 2, 4)),
            dma((2, 2, 4)),
            dma((2, 2, 4)),
            dma((2, 2, 4)),
            dma((2, 2, 4)),
            dma((2, 3, 2)),
            dma((2, 3, 2)),
            dma((3,)),
            dma((3,)),
            dma((3, 3)),
            dma((3, 3)),
            dma((3, 3)),
            dma((3, 4)),
            dma((3, 3)),
            dma((3, 3)),
            dma((16,)),
            dma((1,)),
        ],
        compiler_params=pltpu.CompilerParams(
            collective_id=0,
            has_side_effects=True,
            vmem_limit_bytes=44 * 1024 * 1024,
        ),
        cost_estimate=pl.CostEstimate(flops=3_000_000_000, bytes_accessed=5_000_000, transcendentals=0),
    )(*(pltpu.with_memory_space_constraint(a, pltpu.HBM) for a in operands))


def solution(mesh):
    return jax.shard_map(
        local,
        mesh=mesh,
        in_specs=(
            P("scen", None, "grp"),
            P("scen"),
            P("scen", None, "grp", None),
            P("scen", None, None, "grp", None),
            P("scen", None, None),
        ),
        out_specs=P("grp", "scen"),
        check_vma=False,
    )
```

```python
import math

import jax
import jax.numpy as jnp
from jax import lax
from jax.experimental import pallas as pl
from jax.experimental.pallas import tpu as pltpu
from jax.sharding import PartitionSpec as P

F32 = jnp.float32
BF16 = jnp.bfloat16
MESH = pl.DeviceIdType.MESH

NX = 4
NZ = 4
NY = 4
SB = 256
NS = 4
ROWS = NS * SB
HALF = ROWS // 2
PACK = 9
REL = (0, 1, 3, 2)

BATCHES = (
    ((3, 0), (3, 1), (3, 2), (0, 0), (0, 1), (0, 2)),
    ((1, 0), (1, 1), (1, 2), (2, 0), (2, 1), (2, 2)),
    ((3, 3), (0, 3), (1, 3), (2, 3)),
)
STARTS = (0, 6, 12)
OTHERS = ((0,), (1, 2), (0, 1, 2))
WIDTH = ((0, 1, 2), (0, 1, 2), (3,))
TILES = 16


def send(src, dst, send_sem, recv_sem, device):
    pltpu.make_async_remote_copy(
        src_ref=src,
        dst_ref=dst,
        send_sem=send_sem,
        recv_sem=recv_sem,
        device_id=device,
        device_id_type=MESH,
    ).start()


def await_bytes(ref, sem):
    pltpu.make_async_copy(ref, ref, sem).wait()


def flag(condition):
    return jnp.where(condition, 1.0, 0.0).astype(F32)


def mm(a, b):
    return lax.dot_general(a, b, (((1,), (1,)), ((), ())), preferred_element_type=F32)


def kernel(
    scaling,
    targets_hbm,
    reach_hbm,
    linking_hbm,
    diag,
    off,
    out,
    targets,
    reach,
    linking,
    choice,
    factors,
    lower,
    columns,
    solved,
    raw_z,
    solved_z,
    partial,
    from_core,
    to_y,
    from_y,
    reduced,
    near_z,
    near_x,
    slices,
    final,
    in_s,
    fz_s,
    fz_r,
    fx_s,
    fx_r,
    ff_s,
    ff_r,
    sx_s,
    sx_r,
    zl_s,
    zl_r,
    c_s,
    c_r,
    y_s,
    y_r,
    nz_s,
    nz_r,
    nx_s,
    nx_r,
    fn_s,
    fn_r,
):
    s = lax.axis_index("scen")
    g = lax.axis_index("grp")
    x, z = g // NZ, g % NZ
    core, y, z_hi = s % 2, (s // 2) % NY, s // (2 * NY)
    right_x, left_x, far_x = (x + 1) % NX, (x + 3) % NX, (x + 2) % NX
    right = (s, right_x * NZ + z)
    left = (s, left_x * NZ + z)
    upper = z // 2
    places = (z + 1 - 2 * (z % 2), 2 - upper, 3 - 3 * upper, z)

    def at_x(i):
        return (x + REL[i]) % NX

    barrier = pltpu.get_barrier_semaphore()

    def greet(k, carry):
        pl.semaphore_signal(barrier, inc=1, device_id=((s + k) % 16, g), device_id_type=MESH)
        return carry

    lax.fori_loop(1, 16, greet, 0)
    for k in range(1, NZ):
        pl.semaphore_signal(barrier, inc=1, device_id=(s, x * NZ + (z + k) % NZ), device_id_type=MESH)
    for k in range(1, NX):
        pl.semaphore_signal(barrier, inc=1, device_id=(s, ((x + k) % NX) * NZ + z), device_id_type=MESH)

    fetches = [(targets_hbm, targets), (reach_hbm, reach)]
    for sc in range(2):
        fetches.append((off.at[sc, 2], choice.at[sc]))
        fetches.append((diag.at[sc], factors.at[sc, g, pl.ds(0, NS)]))
        for i in range(2):
            fetches.append((off.at[sc, i], factors.at[sc, g, pl.ds(NS + 2 * i, 2)]))
    fetches.append((linking_hbm, linking))
    copies = [pltpu.make_async_copy(a, b, in_s.at[n]) for n, (a, b) in enumerate(fetches)]
    for copy in copies:
        copy.start()
    for copy in copies[:-1]:
        copy.wait()
    for sc in range(2):
        first = choice[sc, 0].astype(F32) * flag(targets[sc, 0, 2] == 3)
        second = choice[sc, 1].astype(F32) * flag(targets[sc, 1, 2] == 3)
        factors[sc, g, 8] = (first + second).astype(BF16)

    pl.semaphore_wait(barrier, 21)

    def shard(sc, xx, k):
        return factors.at[sc, xx * NZ + (z + k) % NZ]

    def x_send(sc, k):
        piece = shard(sc, x, k)
        send(piece, piece, fx_s.at[sc, 0, k], fx_r.at[sc, 0, k], right)
        send(piece, piece, fx_s.at[sc, 1, k], fx_r.at[sc, 1, k], left)

    def goes_on(q):
        return ((q < z) & (z < NZ - 1), (q > z) & (z > 0))

    def z_take(sc, o):
        q = places[o]
        piece = factors.at[sc, x * NZ + q]
        await_bytes(piece, fz_r.at[sc, q])
        for onward, device in zip(goes_on(q), ((s, g + 1), (s, g - 1))):

            @pl.when(onward)
            def _(device=device):
                send(piece, piece, fz_s.at[sc, 2 + o], fz_r.at[sc, q], device)

        x_send(sc, (q + NZ - z) % NZ)

    def pass_right(sc, k):
        piece = shard(sc, left_x, k)
        await_bytes(piece, fx_r.at[sc, 0, k])
        send(piece, piece, ff_s.at[sc, 0, k], ff_r.at[sc, 0, k], right)

    def pass_left(sc, k):
        piece = shard(sc, right_x, k)
        await_bytes(piece, fx_r.at[sc, 1, k])
        send(piece, piece, ff_s.at[sc, 1, k], ff_r.at[sc, 1, k], left)

    def rest(sc):
        for k in (1, 2):
            await_bytes(shard(sc, left_x, k), fx_r.at[sc, 0, k])
            await_bytes(shard(sc, far_x, k), ff_r.at[sc, 1, k])
        for k in (0, 3):
            await_bytes(shard(sc, right_x, k), fx_r.at[sc, 1, k])
            await_bytes(shard(sc, far_x, k), ff_r.at[sc, 0, k])

    def z_send(sc):
        own = factors.at[sc, g]

        @pl.when(z < NZ - 1)
        def _():
            send(own, own, fz_s.at[sc, 0], fz_r.at[sc, z], (s, g + 1))

        @pl.when(z > 0)
        def _():
            send(own, own, fz_s.at[sc, 1], fz_r.at[sc, z], (s, g - 1))

        x_send(sc, 0)

    def prepare(sc):
        for i in range(3):
            for j in range(i + 1, NS):
                if i == 2:
                    block = factors[sc, :, 8].reshape(SB, SB)
                else:
                    block = jnp.zeros((SB, SB), BF16)
                    for p in range(2):
                        chosen = flag(targets[sc, p, i] == j).astype(BF16)
                        block = block + factors[sc, :, 4 + 2 * i + p].reshape(SB, SB) * chosen
                lower[sc, j - 1, :, i * SB : (i + 1) * SB] = block

    def solve(sc, source, target, own=False, after=None):
        for j in range(NS):
            if own and j == 1:
                prepare(sc)
            here = slice(j * SB, (j + 1) * SB)
            residual = source[:, here].astype(F32) * flag(j >= NS - reach[sc])
            if j:
                residual = residual - mm(target[:, : j * SB], lower[sc, j - 1, :, : j * SB])
            inverse = factors[sc, :, j].reshape(SB, SB)
            target[:, here] = mm(residual.astype(BF16), inverse).astype(BF16)
            if after is not None:
                after(j)

    def x_part(sc, i, form, first=0, count=SB):
        return solved.at[sc, i, pl.ds(first, count), pl.ds(form * HALF, HALF)]

    def solve_own(sc):
        def after(j):
            if j % 2:
                form = j // 2
                own = x_part(sc, 0, form)
                send(own, x_part(sc, 2, form), sx_s.at[sc, form, 0], sx_r.at[sc, form, 0], right)
                send(own, x_part(sc, 1, form), sx_s.at[sc, form, 1], sx_r.at[sc, form, 1], left)

        solve(sc, columns.at[sc], solved.at[sc, 0], True, after)

    def pass_x(sc, form):
        await_bytes(x_part(sc, 2, form), sx_r.at[sc, form, 0])
        send(
            x_part(sc, 2, form, 0, SB // 2),
            x_part(sc, 3, form, 0, SB // 2),
            sx_s.at[sc, form, 2],
            sx_r.at[sc, form, 2],
            right,
        )
        await_bytes(x_part(sc, 1, form), sx_r.at[sc, form, 1])
        send(
            x_part(sc, 1, form, SB // 2, SB // 2),
            x_part(sc, 3, form, SB // 2, SB // 2),
            sx_s.at[sc, form, 3],
            sx_r.at[sc, form, 3],
            left,
        )

    def far(sc, form):
        for n in range(2):
            await_bytes(x_part(sc, 3, form, n * (SB // 2), SB // 2), sx_r.at[sc, form, 2 + n])

    def z_half(ref, h):
        return ref.at[pl.ds(h * (SB // 2), SB // 2)]

    def start_z():
        for h in range(2):

            @pl.when(z < NZ - 1)
            def _(h=h):
                send(z_half(columns.at[0], h), z_half(raw_z.at[z], h), zl_s.at[0, 0, h], zl_r.at[0, 0, h], (s, g + 1))

            @pl.when(z > 0)
            def _(h=h):
                send(z_half(columns.at[1], h), z_half(raw_z.at[z], h), zl_s.at[1, 0, h], zl_r.at[1, 0, h], (s, g - 1))

    def pass_z(k):
        for h in range(2):

            @pl.when(z - k >= 0)
            def _(h=h):
                block = z_half(raw_z.at[z - k], h)
                await_bytes(block, zl_r.at[0, k - 1, h])
                if k < NZ - 1:

                    @pl.when(z < NZ - 1)
                    def _():
                        send(block, block, zl_s.at[0, k, h], zl_r.at[0, k, h], (s, g + 1))

            @pl.when(z + k <= NZ - 1)
            def _(h=h):
                block = z_half(raw_z.at[z + k], h)
                await_bytes(block, zl_r.at[1, k - 1, h])
                if k < NZ - 1:

                    @pl.when(z > 0)
                    def _():
                        send(block, block, zl_s.at[1, k, h], zl_r.at[1, k, h], (s, g - 1))

    def solve_z(o):
        sc = (1 - z % 2) if o == 0 else (1 - upper)
        solve(sc, raw_z.at[places[o]], solved_z.at[places[o]])

    z_send(0)
    z_send(1)
    copies[-1].wait()
    for sc in range(2):
        for j in range(NS):
            block = linking[sc, j * SB : (j + 1) * SB, :].astype(F32)
            columns[sc, :, j * SB : (j + 1) * SB] = block.T.astype(BF16)
    z_take(0, 0)
    z_take(0, 1)
    z_take(1, 0)
    z_take(1, 1)
    pass_right(0, 0)
    pass_right(1, 0)
    z_take(0, 2)
    z_take(1, 2)
    start_z()
    pass_left(0, 1)
    pass_left(0, 2)
    pass_right(0, 3)
    pass_right(1, 3)
    pass_left(1, 1)
    pass_left(1, 2)
    rest(0)
    solve_own(0)
    pass_z(1)
    rest(1)
    solve_own(1)

    def store(n, tile):
        partial[0, n] = tile[: SB // 2]
        partial[1, n] = tile[SB // 2 :]

    def wide(sc):
        return solved[sc, 0:3].reshape(3 * SB, ROWS)

    def store_wide(n, product, axis):
        for i in range(3):
            store(n + i, lax.slice_in_dim(product, i * SB, (i + 1) * SB, axis=axis))

    def pair(first):
        return solved_z[first : first + 2].reshape(2 * SB, ROWS)

    def gram(batch):
        near_below = z % 2 == 1
        below = upper == 1
        if batch == 0:
            store_wide(0, mm(solved[0, 0], wide(0)) + mm(solved[1, 0], wide(1)), 1)

            @pl.when(near_below)
            def _():
                store_wide(3, mm(solved_z[places[0]], wide(0)), 1)

            @pl.when(jnp.logical_not(near_below))
            def _():
                store_wide(3, mm(wide(1), solved_z[places[0]]), 0)
        elif batch == 1:
            @pl.when(below)
            def _():
                product = mm(pair(0), wide(0))
                store_wide(6, product[SB:], 1)
                store_wide(9, product[:SB], 1)

            @pl.when(jnp.logical_not(below))
            def _():
                product = mm(wide(1), pair(2))
                store_wide(6, product[:, :SB], 0)
                store_wide(9, product[:, SB:], 0)
        else:
            store(12, mm(solved[0, 0], solved[0, 3]) + mm(solved[1, 0], solved[1, 3]))

            @pl.when(near_below)
            def _():
                store(13, mm(solved_z[places[0]], solved[0, 3]))

            @pl.when(jnp.logical_not(near_below))
            def _():
                store(13, mm(solved[1, 3], solved_z[places[0]]))

            @pl.when(below)
            def _():
                product = mm(pair(0), solved[0, 3])
                store(14, product[SB:])
                store(15, product[:SB])

            @pl.when(jnp.logical_not(below))
            def _():
                product = mm(solved[1, 3], pair(2))
                store(14, product[:, :SB])
                store(15, product[:, SB:])

    def span(batch):
        return pl.ds(STARTS[batch], len(BATCHES[batch]))

    def to_core(batch):
        send(
            partial.at[1 - core, span(batch)],
            from_core.at[span(batch)],
            c_s.at[batch],
            c_r.at[batch],
            (s + 1 - 2 * core, g),
        )

    def of_y(yy, first=0, count=32):
        return pl.ds(pl.multiple_of((yy % NY) * 32 + first, 16), count)

    def both_cores(n, rows):
        return partial[core, n, rows, :] + from_core[n, rows, :]

    def over_tiles(batch, body):
        def step(n, carry):
            body(n)
            return carry

        lax.fori_loop(STARTS[batch], STARTS[batch] + len(BATCHES[batch]), step, 0)

    def along_y(batch):
        tiles = span(batch)
        await_bytes(from_core.at[tiles], c_r.at[batch])
        for k in (2, 1, 3):

            def body(n, k=k):
                to_y[k - 1, n] = both_cores(n, of_y(y + k)).astype(BF16)

            over_tiles(batch, body)
            send(
                to_y.at[k - 1, tiles],
                from_y.at[k - 1, tiles],
                y_s.at[batch, k - 1],
                y_r.at[batch, k - 1],
                (z_hi * 8 + ((y + k) % NY) * 2 + core, g),
            )

    def finish_y(batch):
        tiles = span(batch)
        for k in range(1, NY):
            await_bytes(from_y.at[k - 1, tiles], y_r.at[batch, k - 1])
        for n, (o, i) in enumerate(BATCHES[batch], STARTS[batch]):
            value = both_cores(n, of_y(y))
            for k in range(1, NY):
                value += from_y[k - 1, n].astype(F32)
            value = value.astype(BF16)
            if o == 3:
                slices[3, i] = value
            else:
                reduced[o, i] = value
                if i == 0:
                    near_x[0, o] = value

    def batch_z(ref, place, batch):
        return ref.at[place, pl.ds(WIDTH[batch][0], len(WIDTH[batch]))]

    def batch_x(ref, place, batch):
        return ref.at[place, pl.ds(OTHERS[batch][0], len(OTHERS[batch]))]

    def to_groups(batch):
        for o in OTHERS[batch]:
            send(
                batch_z(reduced, o, batch),
                batch_z(near_z, z, batch),
                nz_s.at[batch, o],
                nz_r.at[batch, z],
                (s, x * NZ + places[o]),
            )
        for i in WIDTH[batch]:
            if i:
                back = (0, 2, 1, 3)[i]
                send(
                    reduced.at[pl.ds(OTHERS[batch][0], len(OTHERS[batch])), i],
                    batch_x(near_x, back, batch),
                    nx_s.at[batch, i - 1],
                    nx_r.at[batch, back - 1],
                    (s, at_x(i) * NZ + z),
                )

    def from_groups(batch):
        for n, i in enumerate(WIDTH[batch]):
            if i:
                await_bytes(batch_x(near_x, i, batch), nx_r.at[batch, i - 1])
            for o in OTHERS[batch]:
                if n == 0:
                    await_bytes(batch_z(near_z, places[o], batch), nz_r.at[batch, places[o]])
                deliver(o, i)

    out_rows = pl.ds(pl.multiple_of(core * 128 + y * 32, 32), 32)

    def deliver(o, i):
        if o < 3:
            both = near_z[places[o], i].astype(F32) + near_x[i, o].astype(F32)
            slices[o, i] = both.astype(BF16)
        b = at_x(i) * NZ + places[o]
        piece = slices.at[o, i]
        target = final.at[z_hi, out_rows]

        @pl.when(b == s)
        def _():
            pltpu.make_async_copy(piece, target, fn_r.at[0]).start()

        @pl.when(b != s)
        def _():
            send(piece, target, fn_s.at[o * 4 + i], fn_r.at[0], (b, g))

    pass_z(2)
    solve_z(0)
    pass_x(0, 0)
    solve_z(1)
    pass_x(0, 1)
    pass_x(1, 0)
    pass_x(1, 1)
    gram(0)
    to_core(0)
    pass_z(3)
    solve_z(2)
    along_y(0)
    gram(1)
    to_core(1)
    far(0, 0)
    far(0, 1)
    along_y(1)
    far(1, 0)
    far(1, 1)
    gram(2)
    to_core(2)
    finish_y(0)
    to_groups(0)
    for i in range(3):
        deliver(3, i)
    along_y(2)
    from_groups(0)
    finish_y(1)
    to_groups(1)
    finish_y(2)
    to_groups(2)
    from_groups(1)
    deliver(3, 3)
    from_groups(2)

    for sc in range(2):

        @pl.when(z < NZ - 1)
        def _(sc=sc):
            await_bytes(factors.at[sc, g], fz_s.at[sc, 0])

        @pl.when(z > 0)
        def _(sc=sc):
            await_bytes(factors.at[sc, g], fz_s.at[sc, 1])

        for o in range(3):
            for onward in goes_on(places[o]):

                @pl.when(onward)
                def _(sc=sc, o=o):
                    await_bytes(factors.at[sc, g], fz_s.at[sc, 2 + o])

        for d in range(2):
            for k in range(4):
                await_bytes(factors.at[sc, g], fx_s.at[sc, d, k])
            for k in ((0, 3), (1, 2))[d]:
                await_bytes(factors.at[sc, g], ff_s.at[sc, d, k])
            for n in range(2):
                await_bytes(x_part(sc, 0, d), sx_s.at[sc, d, n])
                await_bytes(x_part(sc, 0, d, 0, SB // 2), sx_s.at[sc, d, 2 + n])
    for k in range(NZ - 1):

        @pl.when((z - k >= 0) & (z < NZ - 1))
        def _(k=k):
            for h in range(2):
                await_bytes(z_half(raw_z.at[0], h), zl_s.at[0, k, h])

        @pl.when((z + k <= NZ - 1) & (z > 0))
        def _(k=k):
            for h in range(2):
                await_bytes(z_half(raw_z.at[0], h), zl_s.at[1, k, h])

    for batch in range(3):
        await_bytes(from_core.at[span(batch)], c_s.at[batch])
    for batch in range(3):
        for k in range(NY - 1):
            await_bytes(from_y.at[k, span(batch)], y_s.at[batch, k])
    for batch in range(3):
        for o in OTHERS[batch]:
            await_bytes(batch_z(near_z, 0, batch), nz_s.at[batch, o])
        for i in WIDTH[batch]:
            if i:
                await_bytes(batch_x(near_x, 0, batch), nx_s.at[batch, i - 1])
    await_bytes(final, fn_r.at[0])

    @pl.when(z > s % NZ)
    def _():
        out[...] = ((final[0].astype(F32) + final[1].astype(F32)) * scaling).T

    @pl.when(z <= s % NZ)
    def _():
        out[...] = (final[0].astype(F32) + final[1].astype(F32)) * scaling

    for o in range(4):
        for i in range(4):

            @pl.when(at_x(i) * NZ + places[o] != s)
            def _(o=o, i=i):
                await_bytes(slices.at[0, 0], fn_s.at[o * 4 + i])


def local(linking, reach_count, diag_inverse, off_blocks, targets):
    scaling = 1.0 / math.sqrt(linking.shape[0] * 16 * ROWS)
    dma = pltpu.SemaphoreType.DMA
    vmem = pl.BlockSpec(memory_space=pltpu.VMEM)
    hbm = pl.BlockSpec(memory_space=pltpu.HBM)

    def body(*refs):
        kernel(scaling, *refs)

    operands = (jnp.swapaxes(targets, 1, 2), reach_count, linking, diag_inverse, off_blocks)
    return pl.pallas_call(
        body,
        out_shape=jax.ShapeDtypeStruct((SB, SB), F32),
        in_specs=[hbm] * 5,
        out_specs=vmem,
        scratch_shapes=[
            pltpu.SMEM((2, 2, NS), jnp.int32),
            pltpu.SMEM((2,), jnp.int32),
            pltpu.VMEM((2, ROWS, SB), BF16),
            pltpu.VMEM((2, 2, 16, SB), BF16),
            pltpu.VMEM((2, 16, PACK, 16, SB), BF16),
            pltpu.VMEM((2, NS - 1, SB, 3 * SB), BF16),
            pltpu.VMEM((2, SB, ROWS), BF16),
            pltpu.VMEM((2, NX, SB, ROWS), BF16),
            pltpu.VMEM((NZ, SB, ROWS), BF16),
            pltpu.VMEM((NZ, SB, ROWS), BF16),
            pltpu.VMEM((2, TILES, SB // 2, SB), F32),
            pltpu.VMEM((TILES, SB // 2, SB), F32),
            pltpu.VMEM((NY - 1, TILES, 32, SB), BF16),
            pltpu.VMEM((NY - 1, TILES, 32, SB), BF16),
            pltpu.VMEM((3, NX, 32, SB), BF16),
            pltpu.VMEM((NZ, NX, 32, SB), BF16),
            pltpu.VMEM((NX, 3, 32, SB), BF16),
            pltpu.VMEM((4, NX, 32, SB), BF16),
            pltpu.VMEM((2, SB, SB), BF16),
            dma((11,)),
            dma((2, 5)),
            dma((2, 4)),
            dma((2, 2, 4)),
            dma((2, 2, 4)),
            dma((2, 2, 4)),
            dma((2, 2, 4)),
            dma((2, 2, 4)),
            dma((2, 2, 4)),
            dma((2, 3, 2)),
            dma((2, 3, 2)),
            dma((3,)),
            dma((3,)),
            dma((3, 3)),
            dma((3, 3)),
            dma((3, 3)),
            dma((3, 4)),
            dma((3, 3)),
            dma((3, 3)),
            dma((16,)),
            dma((1,)),
        ],
        compiler_params=pltpu.CompilerParams(
            collective_id=0,
            has_side_effects=True,
            vmem_limit_bytes=44 * 1024 * 1024,
        ),
        cost_estimate=pl.CostEstimate(flops=3_000_000_000, bytes_accessed=5_000_000, transcendentals=0),
    )(*(pltpu.with_memory_space_constraint(a, pltpu.HBM) for a in operands))


def solution(mesh):
    return jax.shard_map(
        local,
        mesh=mesh,
        in_specs=(
            P("scen", None, "grp"),
            P("scen"),
            P("scen", None, "grp", None),
            P("scen", None, None, "grp", None),
            P("scen", None, None),
        ),
        out_specs=P("grp", "scen"),
        check_vma=False,
    )
```

```python
import math

import jax
import jax.numpy as jnp
from jax import lax
from jax.experimental import pallas as pl
from jax.experimental.pallas import tpu as pltpu
from jax.sharding import PartitionSpec as P

F32 = jnp.float32
BF16 = jnp.bfloat16
MESH = pl.DeviceIdType.MESH

NX = 4
NZ = 4
NY = 4
SB = 256
NS = 4
ROWS = NS * SB
HALF = ROWS // 2
PACK = 9
REL = (0, 1, 3, 2)

BATCHES = (
    ((3, 0), (3, 1), (3, 2), (0, 0), (0, 1), (0, 2)),
    ((1, 0), (1, 1), (1, 2), (2, 0), (2, 1), (2, 2)),
    ((3, 3), (0, 3), (1, 3), (2, 3)),
)
STARTS = (0, 6, 12)
OTHERS = ((0,), (1, 2), (0, 1, 2))
WIDTH = ((0, 1, 2), (0, 1, 2), (3,))
TILES = 16


def send(src, dst, send_sem, recv_sem, device):
    pltpu.make_async_remote_copy(
        src_ref=src,
        dst_ref=dst,
        send_sem=send_sem,
        recv_sem=recv_sem,
        device_id=device,
        device_id_type=MESH,
    ).start()


def await_bytes(ref, sem):
    pltpu.make_async_copy(ref, ref, sem).wait()


def flag(condition):
    return jnp.where(condition, 1.0, 0.0).astype(F32)


def mm(a, b):
    return lax.dot_general(a, b, (((1,), (1,)), ((), ())), preferred_element_type=F32)


def kernel(
    scaling,
    targets_hbm,
    reach_hbm,
    linking_hbm,
    diag,
    off,
    out,
    targets,
    reach,
    linking,
    choice,
    factors,
    lower,
    columns,
    solved,
    raw_z,
    solved_z,
    partial,
    from_core,
    to_y,
    from_y,
    reduced,
    near_z,
    near_x,
    slices,
    final,
    in_s,
    fz_s,
    fz_r,
    fx_s,
    fx_r,
    ff_s,
    ff_r,
    sx_s,
    sx_r,
    zl_s,
    zl_r,
    c_s,
    c_r,
    y_s,
    y_r,
    nz_s,
    nz_r,
    nx_s,
    nx_r,
    fn_s,
    fn_r,
):
    s = lax.axis_index("scen")
    g = lax.axis_index("grp")
    x, z = g // NZ, g % NZ
    core, y, z_hi = s % 2, (s // 2) % NY, s // (2 * NY)
    right_x, left_x, far_x = (x + 1) % NX, (x + 3) % NX, (x + 2) % NX
    right = (s, right_x * NZ + z)
    left = (s, left_x * NZ + z)
    upper = z // 2
    places = (z + 1 - 2 * (z % 2), 2 - upper, 3 - 3 * upper, z)

    def at_x(i):
        return (x + REL[i]) % NX

    barrier = pltpu.get_barrier_semaphore()

    def greet(k, carry):
        pl.semaphore_signal(barrier, inc=1, device_id=((s + k) % 16, g), device_id_type=MESH)
        return carry

    lax.fori_loop(1, 16, greet, 0)
    for k in range(1, NZ):
        pl.semaphore_signal(barrier, inc=1, device_id=(s, x * NZ + (z + k) % NZ), device_id_type=MESH)
    for k in range(1, NX):
        pl.semaphore_signal(barrier, inc=1, device_id=(s, ((x + k) % NX) * NZ + z), device_id_type=MESH)

    fetches = [(targets_hbm, targets), (reach_hbm, reach)]
    for sc in range(2):
        fetches.append((off.at[sc, 2], choice.at[sc]))
        fetches.append((diag.at[sc], factors.at[sc, g, pl.ds(0, NS)]))
        for i in range(2):
            fetches.append((off.at[sc, i], factors.at[sc, g, pl.ds(NS + 2 * i, 2)]))
    fetches.append((linking_hbm, linking))
    copies = [pltpu.make_async_copy(a, b, in_s.at[n]) for n, (a, b) in enumerate(fetches)]
    for copy in copies:
        copy.start()
    for copy in copies[:-1]:
        copy.wait()
    for sc in range(2):
        first = choice[sc, 0].astype(F32) * flag(targets[sc, 0, 2] == 3)
        second = choice[sc, 1].astype(F32) * flag(targets[sc, 1, 2] == 3)
        factors[sc, g, 8] = (first + second).astype(BF16)

    pl.semaphore_wait(barrier, 21)

    def shard(sc, xx, k):
        return factors.at[sc, xx * NZ + (z + k) % NZ]

    def x_send(sc, k):
        piece = shard(sc, x, k)
        send(piece, piece, fx_s.at[sc, 0, k], fx_r.at[sc, 0, k], right)
        send(piece, piece, fx_s.at[sc, 1, k], fx_r.at[sc, 1, k], left)

    def goes_on(q):
        return ((q < z) & (z < NZ - 1), (q > z) & (z > 0))

    def z_take(sc, o):
        q = places[o]
        piece = factors.at[sc, x * NZ + q]
        await_bytes(piece, fz_r.at[sc, q])
        for onward, device in zip(goes_on(q), ((s, g + 1), (s, g - 1))):

            @pl.when(onward)
            def _(device=device):
                send(piece, piece, fz_s.at[sc, 2 + o], fz_r.at[sc, q], device)

        x_send(sc, (q + NZ - z) % NZ)

    def pass_right(sc, k):
        piece = shard(sc, left_x, k)
        await_bytes(piece, fx_r.at[sc, 0, k])
        send(piece, piece, ff_s.at[sc, 0, k], ff_r.at[sc, 0, k], right)

    def pass_left(sc, k):
        piece = shard(sc, right_x, k)
        await_bytes(piece, fx_r.at[sc, 1, k])
        send(piece, piece, ff_s.at[sc, 1, k], ff_r.at[sc, 1, k], left)

    def rest(sc):
        for k in (1, 2):
            await_bytes(shard(sc, left_x, k), fx_r.at[sc, 0, k])
            await_bytes(shard(sc, far_x, k), ff_r.at[sc, 1, k])
        for k in (0, 3):
            await_bytes(shard(sc, right_x, k), fx_r.at[sc, 1, k])
            await_bytes(shard(sc, far_x, k), ff_r.at[sc, 0, k])

    def z_send(sc):
        own = factors.at[sc, g]

        @pl.when(z < NZ - 1)
        def _():
            send(own, own, fz_s.at[sc, 0], fz_r.at[sc, z], (s, g + 1))

        @pl.when(z > 0)
        def _():
            send(own, own, fz_s.at[sc, 1], fz_r.at[sc, z], (s, g - 1))

        x_send(sc, 0)

    def prepare(sc):
        for i in range(3):
            for j in range(i + 1, NS):
                if i == 2:
                    block = factors[sc, :, 8].reshape(SB, SB)
                else:
                    block = jnp.zeros((SB, SB), BF16)
                    for p in range(2):
                        chosen = flag(targets[sc, p, i] == j).astype(BF16)
                        block = block + factors[sc, :, 4 + 2 * i + p].reshape(SB, SB) * chosen
                lower[sc, j - 1, :, i * SB : (i + 1) * SB] = block

    def solve(sc, source, target, own=False, after=None):
        for j in range(NS):
            if own and j == 1:
                prepare(sc)
            here = slice(j * SB, (j + 1) * SB)
            residual = source[:, here].astype(F32) * flag(j >= NS - reach[sc])
            if j:
                residual = residual - mm(target[:, : j * SB], lower[sc, j - 1, :, : j * SB])
            inverse = factors[sc, :, j].reshape(SB, SB)
            target[:, here] = mm(residual.astype(BF16), inverse).astype(BF16)
            if after is not None:
                after(j)

    def x_part(sc, i, form, first=0, count=SB):
        return solved.at[sc, i, pl.ds(first, count), pl.ds(form * HALF, HALF)]

    def solve_own(sc):
        def after(j):
            if j % 2:
                form = j // 2
                own = x_part(sc, 0, form)
                send(own, x_part(sc, 2, form), sx_s.at[sc, form, 0], sx_r.at[sc, form, 0], right)
                send(own, x_part(sc, 1, form), sx_s.at[sc, form, 1], sx_r.at[sc, form, 1], left)

        solve(sc, columns.at[sc], solved.at[sc, 0], True, after)

    def pass_x(sc, form):
        await_bytes(x_part(sc, 2, form), sx_r.at[sc, form, 0])
        send(
            x_part(sc, 2, form, 0, SB // 2),
            x_part(sc, 3, form, 0, SB // 2),
            sx_s.at[sc, form, 2],
            sx_r.at[sc, form, 2],
            right,
        )
        await_bytes(x_part(sc, 1, form), sx_r.at[sc, form, 1])
        send(
            x_part(sc, 1, form, SB // 2, SB // 2),
            x_part(sc, 3, form, SB // 2, SB // 2),
            sx_s.at[sc, form, 3],
            sx_r.at[sc, form, 3],
            left,
        )

    def far(sc, form):
        for n in range(2):
            await_bytes(x_part(sc, 3, form, n * (SB // 2), SB // 2), sx_r.at[sc, form, 2 + n])

    def z_half(ref, h):
        return ref.at[pl.ds(h * (SB // 2), SB // 2)]

    def start_z():
        for h in range(2):

            @pl.when(z < NZ - 1)
            def _(h=h):
                send(z_half(columns.at[0], h), z_half(raw_z.at[z], h), zl_s.at[0, 0, h], zl_r.at[0, 0, h], (s, g + 1))

            @pl.when(z > 0)
            def _(h=h):
                send(z_half(columns.at[1], h), z_half(raw_z.at[z], h), zl_s.at[1, 0, h], zl_r.at[1, 0, h], (s, g - 1))

    def pass_z(k):
        for h in range(2):

            @pl.when(z - k >= 0)
            def _(h=h):
                block = z_half(raw_z.at[z - k], h)
                await_bytes(block, zl_r.at[0, k - 1, h])
                if k < NZ - 1:

                    @pl.when(z < NZ - 1)
                    def _():
                        send(block, block, zl_s.at[0, k, h], zl_r.at[0, k, h], (s, g + 1))

            @pl.when(z + k <= NZ - 1)
            def _(h=h):
                block = z_half(raw_z.at[z + k], h)
                await_bytes(block, zl_r.at[1, k - 1, h])
                if k < NZ - 1:

                    @pl.when(z > 0)
                    def _():
                        send(block, block, zl_s.at[1, k, h], zl_r.at[1, k, h], (s, g - 1))

    def solve_z(o):
        sc = (1 - z % 2) if o == 0 else (1 - upper)
        solve(sc, raw_z.at[places[o]], solved_z.at[places[o]])

    z_send(0)
    z_send(1)
    copies[-1].wait()
    for sc in range(2):
        for j in range(NS):
            block = linking[sc, j * SB : (j + 1) * SB, :].astype(F32)
            columns[sc, :, j * SB : (j + 1) * SB] = block.T.astype(BF16)
    z_take(0, 0)
    z_take(0, 1)
    pass_right(0, 0)
    z_take(0, 2)
    z_take(1, 0)
    z_take(1, 1)
    z_take(1, 2)
    start_z()
    pass_left(0, 1)
    pass_left(0, 2)
    pass_right(0, 3)
    pass_right(1, 3)
    pass_left(1, 1)
    pass_right(1, 0)
    pass_left(1, 2)
    rest(0)
    solve_own(0)
    pass_z(1)
    rest(1)
    solve_own(1)

    def store(n, tile):
        partial[0, n] = tile[: SB // 2]
        partial[1, n] = tile[SB // 2 :]

    def wide(sc):
        return solved[sc, 0:3].reshape(3 * SB, ROWS)

    def store_wide(n, product, axis):
        for i in range(3):
            store(n + i, lax.slice_in_dim(product, i * SB, (i + 1) * SB, axis=axis))

    def pair(first):
        return solved_z[first : first + 2].reshape(2 * SB, ROWS)

    def gram(batch):
        near_below = z % 2 == 1
        below = upper == 1
        if batch == 0:
            store_wide(0, mm(solved[0, 0], wide(0)) + mm(solved[1, 0], wide(1)), 1)

            @pl.when(near_below)
            def _():
                store_wide(3, mm(solved_z[places[0]], wide(0)), 1)

            @pl.when(jnp.logical_not(near_below))
            def _():
                store_wide(3, mm(wide(1), solved_z[places[0]]), 0)
        elif batch == 1:
            @pl.when(below)
            def _():
                product = mm(pair(0), wide(0))
                store_wide(6, product[SB:], 1)
                store_wide(9, product[:SB], 1)

            @pl.when(jnp.logical_not(below))
            def _():
                product = mm(wide(1), pair(2))
                store_wide(6, product[:, :SB], 0)
                store_wide(9, product[:, SB:], 0)
        else:
            store(12, mm(solved[0, 0], solved[0, 3]) + mm(solved[1, 0], solved[1, 3]))

            @pl.when(near_below)
            def _():
                store(13, mm(solved_z[places[0]], solved[0, 3]))

            @pl.when(jnp.logical_not(near_below))
            def _():
                store(13, mm(solved[1, 3], solved_z[places[0]]))

            @pl.when(below)
            def _():
                product = mm(pair(0), solved[0, 3])
                store(14, product[SB:])
                store(15, product[:SB])

            @pl.when(jnp.logical_not(below))
            def _():
                product = mm(solved[1, 3], pair(2))
                store(14, product[:, :SB])
                store(15, product[:, SB:])

    def span(batch):
        return pl.ds(STARTS[batch], len(BATCHES[batch]))

    def to_core(batch):
        send(
            partial.at[1 - core, span(batch)],
            from_core.at[span(batch)],
            c_s.at[batch],
            c_r.at[batch],
            (s + 1 - 2 * core, g),
        )

    def of_y(yy, first=0, count=32):
        return pl.ds(pl.multiple_of((yy % NY) * 32 + first, 16), count)

    def both_cores(n, rows):
        return partial[core, n, rows, :] + from_core[n, rows, :]

    def over_tiles(batch, body):
        def step(n, carry):
            body(n)
            return carry

        lax.fori_loop(STARTS[batch], STARTS[batch] + len(BATCHES[batch]), step, 0)

    def along_y(batch):
        tiles = span(batch)
        await_bytes(from_core.at[tiles], c_r.at[batch])
        for k in (2, 1, 3):

            def body(n, k=k):
                to_y[k - 1, n] = both_cores(n, of_y(y + k)).astype(BF16)

            over_tiles(batch, body)
            send(
                to_y.at[k - 1, tiles],
                from_y.at[k - 1, tiles],
                y_s.at[batch, k - 1],
                y_r.at[batch, k - 1],
                (z_hi * 8 + ((y + k) % NY) * 2 + core, g),
            )

    def finish_y(batch):
        tiles = span(batch)
        for k in range(1, NY):
            await_bytes(from_y.at[k - 1, tiles], y_r.at[batch, k - 1])
        for n, (o, i) in enumerate(BATCHES[batch], STARTS[batch]):
            value = both_cores(n, of_y(y))
            for k in range(1, NY):
                value += from_y[k - 1, n].astype(F32)
            value = value.astype(BF16)
            if o == 3:
                slices[3, i] = value
            else:
                reduced[o, i] = value
                if i == 0:
                    near_x[0, o] = value

    def batch_z(ref, place, batch):
        return ref.at[place, pl.ds(WIDTH[batch][0], len(WIDTH[batch]))]

    def batch_x(ref, place, batch):
        return ref.at[place, pl.ds(OTHERS[batch][0], len(OTHERS[batch]))]

    def to_groups(batch):
        for o in OTHERS[batch]:
            send(
                batch_z(reduced, o, batch),
                batch_z(near_z, z, batch),
                nz_s.at[batch, o],
                nz_r.at[batch, z],
                (s, x * NZ + places[o]),
            )
        for i in WIDTH[batch]:
            if i:
                back = (0, 2, 1, 3)[i]
                send(
                    reduced.at[pl.ds(OTHERS[batch][0], len(OTHERS[batch])), i],
                    batch_x(near_x, back, batch),
                    nx_s.at[batch, i - 1],
                    nx_r.at[batch, back - 1],
                    (s, at_x(i) * NZ + z),
                )

    def from_groups(batch):
        for n, i in enumerate(WIDTH[batch]):
            if i:
                await_bytes(batch_x(near_x, i, batch), nx_r.at[batch, i - 1])
            for o in OTHERS[batch]:
                if n == 0:
                    await_bytes(batch_z(near_z, places[o], batch), nz_r.at[batch, places[o]])
                deliver(o, i)

    out_rows = pl.ds(pl.multiple_of(core * 128 + y * 32, 32), 32)

    def deliver(o, i):
        if o < 3:
            both = near_z[places[o], i].astype(F32) + near_x[i, o].astype(F32)
            slices[o, i] = both.astype(BF16)
        b = at_x(i) * NZ + places[o]
        piece = slices.at[o, i]
        target = final.at[z_hi, out_rows]

        @pl.when(b == s)
        def _():
            pltpu.make_async_copy(piece, target, fn_r.at[0]).start()

        @pl.when(b != s)
        def _():
            send(piece, target, fn_s.at[o * 4 + i], fn_r.at[0], (b, g))

    pass_z(2)
    solve_z(0)
    pass_x(0, 0)
    solve_z(1)
    pass_x(0, 1)
    pass_x(1, 0)
    pass_x(1, 1)
    gram(0)
    to_core(0)
    pass_z(3)
    solve_z(2)
    along_y(0)
    gram(1)
    to_core(1)
    far(0, 0)
    far(0, 1)
    along_y(1)
    far(1, 0)
    far(1, 1)
    gram(2)
    to_core(2)
    finish_y(0)
    to_groups(0)
    for i in range(3):
        deliver(3, i)
    along_y(2)
    from_groups(0)
    finish_y(1)
    to_groups(1)
    finish_y(2)
    to_groups(2)
    from_groups(1)
    deliver(3, 3)
    from_groups(2)

    for sc in range(2):

        @pl.when(z < NZ - 1)
        def _(sc=sc):
            await_bytes(factors.at[sc, g], fz_s.at[sc, 0])

        @pl.when(z > 0)
        def _(sc=sc):
            await_bytes(factors.at[sc, g], fz_s.at[sc, 1])

        for o in range(3):
            for onward in goes_on(places[o]):

                @pl.when(onward)
                def _(sc=sc, o=o):
                    await_bytes(factors.at[sc, g], fz_s.at[sc, 2 + o])

        for d in range(2):
            for k in range(4):
                await_bytes(factors.at[sc, g], fx_s.at[sc, d, k])
            for k in ((0, 3), (1, 2))[d]:
                await_bytes(factors.at[sc, g], ff_s.at[sc, d, k])
            for n in range(2):
                await_bytes(x_part(sc, 0, d), sx_s.at[sc, d, n])
                await_bytes(x_part(sc, 0, d, 0, SB // 2), sx_s.at[sc, d, 2 + n])
    for k in range(NZ - 1):

        @pl.when((z - k >= 0) & (z < NZ - 1))
        def _(k=k):
            for h in range(2):
                await_bytes(z_half(raw_z.at[0], h), zl_s.at[0, k, h])

        @pl.when((z + k <= NZ - 1) & (z > 0))
        def _(k=k):
            for h in range(2):
                await_bytes(z_half(raw_z.at[0], h), zl_s.at[1, k, h])

    for batch in range(3):
        await_bytes(from_core.at[span(batch)], c_s.at[batch])
    for batch in range(3):
        for k in range(NY - 1):
            await_bytes(from_y.at[k, span(batch)], y_s.at[batch, k])
    for batch in range(3):
        for o in OTHERS[batch]:
            await_bytes(batch_z(near_z, 0, batch), nz_s.at[batch, o])
        for i in WIDTH[batch]:
            if i:
                await_bytes(batch_x(near_x, 0, batch), nx_s.at[batch, i - 1])
    await_bytes(final, fn_r.at[0])

    @pl.when(z > s % NZ)
    def _():
        out[...] = ((final[0].astype(F32) + final[1].astype(F32)) * scaling).T

    @pl.when(z <= s % NZ)
    def _():
        out[...] = (final[0].astype(F32) + final[1].astype(F32)) * scaling

    for o in range(4):
        for i in range(4):

            @pl.when(at_x(i) * NZ + places[o] != s)
            def _(o=o, i=i):
                await_bytes(slices.at[0, 0], fn_s.at[o * 4 + i])


def local(linking, reach_count, diag_inverse, off_blocks, targets):
    scaling = 1.0 / math.sqrt(linking.shape[0] * 16 * ROWS)
    dma = pltpu.SemaphoreType.DMA
    vmem = pl.BlockSpec(memory_space=pltpu.VMEM)
    hbm = pl.BlockSpec(memory_space=pltpu.HBM)

    def body(*refs):
        kernel(scaling, *refs)

    operands = (jnp.swapaxes(targets, 1, 2), reach_count, linking, diag_inverse, off_blocks)
    return pl.pallas_call(
        body,
        out_shape=jax.ShapeDtypeStruct((SB, SB), F32),
        in_specs=[hbm] * 5,
        out_specs=vmem,
        scratch_shapes=[
            pltpu.SMEM((2, 2, NS), jnp.int32),
            pltpu.SMEM((2,), jnp.int32),
            pltpu.VMEM((2, ROWS, SB), BF16),
            pltpu.VMEM((2, 2, 16, SB), BF16),
            pltpu.VMEM((2, 16, PACK, 16, SB), BF16),
            pltpu.VMEM((2, NS - 1, SB, 3 * SB), BF16),
            pltpu.VMEM((2, SB, ROWS), BF16),
            pltpu.VMEM((2, NX, SB, ROWS), BF16),
            pltpu.VMEM((NZ, SB, ROWS), BF16),
            pltpu.VMEM((NZ, SB, ROWS), BF16),
            pltpu.VMEM((2, TILES, SB // 2, SB), F32),
            pltpu.VMEM((TILES, SB // 2, SB), F32),
            pltpu.VMEM((NY - 1, TILES, 32, SB), BF16),
            pltpu.VMEM((NY - 1, TILES, 32, SB), BF16),
            pltpu.VMEM((3, NX, 32, SB), BF16),
            pltpu.VMEM((NZ, NX, 32, SB), BF16),
            pltpu.VMEM((NX, 3, 32, SB), BF16),
            pltpu.VMEM((4, NX, 32, SB), BF16),
            pltpu.VMEM((2, SB, SB), BF16),
            dma((11,)),
            dma((2, 5)),
            dma((2, 4)),
            dma((2, 2, 4)),
            dma((2, 2, 4)),
            dma((2, 2, 4)),
            dma((2, 2, 4)),
            dma((2, 2, 4)),
            dma((2, 2, 4)),
            dma((2, 3, 2)),
            dma((2, 3, 2)),
            dma((3,)),
            dma((3,)),
            dma((3, 3)),
            dma((3, 3)),
            dma((3, 3)),
            dma((3, 4)),
            dma((3, 3)),
            dma((3, 3)),
            dma((16,)),
            dma((1,)),
        ],
        compiler_params=pltpu.CompilerParams(
            collective_id=0,
            has_side_effects=True,
            vmem_limit_bytes=44 * 1024 * 1024,
        ),
        cost_estimate=pl.CostEstimate(flops=3_000_000_000, bytes_accessed=5_000_000, transcendentals=0),
    )(*(pltpu.with_memory_space_constraint(a, pltpu.HBM) for a in operands))


def solution(mesh):
    return jax.shard_map(
        local,
        mesh=mesh,
        in_specs=(
            P("scen", None, "grp"),
            P("scen"),
            P("scen", None, "grp", None),
            P("scen", None, None, "grp", None),
            P("scen", None, None),
        ),
        out_specs=P("grp", "scen"),
        check_vma=False,
    )
```
